128 devices in a mesh: row: 8 (over x_hi, y), col: 16 (over x_lo, z, core).
Axes of the slice: x: 4 (x_hi: 2, x_lo: 2; x = x_hi * 2 + x_lo), y: 4, z: 4, core: 2. Of those that a mesh axis runs over, the one named last changes fastest.
Arguments:
- vectors: float32 [100352, 2048], P(None, ('row', 'col')), may hold values from -6 to 6
- panels: float32 [2, 100352, 256], P(None, ('row', 'col')), may hold values from -0.078125 to 0.078125
- offsets: int32 [2], replicated, may hold values from 0 to 100096
- factor_upper: float32 [2, 256, 256], replicated, may hold values from -1 to 1
- scales: float32 [2, 256], replicated, may hold values from 1 to 2
Outputs:
- grid_vectors: float32 [100352, 2048], P('row', 'col')
The draws below stay inside these ranges and needn't reach their ends.
All inputs are finite; a program needn't handle non-finite values.
Results may differ from the reference program's by a relative error of at most 0.00015.
Values sent between devices are 32-bit elements; how exact they have to be, the bound alone decides.
No kernel may reach another device: no remote copies, remote signals or barrier semaphores. Data moves between devices by JAX's collectives and lax.ppermute only.
A program may use at most 192 MiB of HBM per device.

```python
import jax
import jax.numpy as jnp
from jax import lax

NROWS = 100352
PW = 256
NB = 64
PROWS = 8
PCOLS = 16
BLOCKS = 196
SLIM = 16
COLS = 2048


def level_of(key, dims, split, least, top_value):
    def one(position, blocks):
        heights = jax.random.uniform(jax.random.fold_in(jax.random.fold_in(key, 6), position), (blocks,), jnp.float32, least / len(split), top_value / len(split))
        return jnp.repeat(jnp.exp(heights), dims[position] // blocks).reshape((-1,) + (1,) * (len(dims) - position - 1))

    gain = one(*split[0])
    for cut in split[1:]:
        gain = gain * one(*cut)
    return gain


def gaussian(own_key, shape, spread, bound, split=(), kind=jnp.bfloat16):
    drawn = jax.random.normal(own_key, shape, jnp.float32) * spread
    if len(split) > 0:
        drawn = level_of(own_key, shape, split, -0.22, 0.18) * drawn
    return jnp.clip(drawn, min=-bound, max=bound).astype(kind)


def setup_inputs(seed: int = 0) -> dict:
    arg_keys = jax.random.split(jax.random.key(seed), 6)
    return {
        "vectors": gaussian(arg_keys[0], (NROWS, COLS), 1.0, 6.0, ((1, 128),), jnp.float32),
        "panels": gaussian(arg_keys[1], (2, NROWS, PW), (NROWS // 16) ** -0.5, 0.078125, ((1, 128),), jnp.float32),
        "offsets": jax.random.randint(arg_keys[2], (2,), 0, NROWS - PW + 1).astype(jnp.int32),
        "factor_upper": gaussian(arg_keys[3], (2, PW, PW), 0.0625, 1.0, (), jnp.float32),
        "scales": jnp.clip(jax.random.uniform(arg_keys[4], (2, PW), jnp.float32, 1.0, 2.0), 1.0, 2.0),
    }


def exact_dot(left, right):
    return jnp.dot(left, right, precision=lax.Precision.HIGHEST, preferred_element_type=jnp.float32)


def inner_dot(left, right):
    return lax.dot_general(left, right, (((0,), (0,)), ((), ())), precision=lax.Precision.HIGHEST, preferred_element_type=jnp.float32)


def reflectors(panels, global_rows, offsets):
    width = panels.shape[2]
    begins = offsets[:, None, None] + jnp.arange(width, dtype=jnp.int32)[None, None, :]
    rows_at = global_rows[None, :, None]
    return jnp.where(rows_at < begins, jnp.float32(0.0), jnp.where(rows_at == begins, jnp.float32(1.0), panels))


def build_factors(factor_upper, scales):
    width = factor_upper.shape[1]
    return jnp.triu(factor_upper, 1) + scales[:, :, None] * jnp.eye(width, dtype=jnp.float32)[None]


def reference(vectors, panels, offsets, factor_upper, scales):
    natural = panels.reshape(2, PROWS, BLOCKS, NB, PW).transpose(0, 2, 1, 3, 4).reshape(2, NROWS, PW)
    reflect = reflectors(natural, jnp.arange(NROWS, dtype=jnp.int32), offsets)
    factors = build_factors(factor_upper, scales)
    current = vectors
    for which in range(2):
        summed = inner_dot(reflect[which], current)
        current = current - exact_dot(reflect[which], exact_dot(factors[which], summed))
    current = current.reshape(BLOCKS, PROWS, NB, COLS).transpose(1, 0, 2, 3).reshape(NROWS, COLS)
    current = current.reshape(NROWS, PROWS, PCOLS, SLIM).transpose(0, 2, 1, 3).reshape(NROWS, COLS)
    return current
```

```python
import jax
import jax.numpy as jnp
from jax import lax
from jax.experimental import pallas as pl
from jax.experimental.pallas import tpu as pltpu
from jax.sharding import PartitionSpec as P

NB = 64
F32 = jnp.float32
BF16 = jnp.bfloat16


def exact_dot(left, right):
    return jnp.dot(left, right, precision=lax.Precision.HIGHEST, preferred_element_type=F32)


def build_factors(factor_upper, scales):
    width = factor_upper.shape[1]
    return jnp.triu(factor_upper, 1) + scales[:, :, None] * jnp.eye(width, dtype=F32)[None]


def split(value):
    high = value.astype(BF16)
    return high, (value - high.astype(F32)).astype(BF16)


def masked(block, offset, row_index, grid_rows, first):
    rows, width = block.shape
    position = first + lax.broadcasted_iota(jnp.int32, (rows, 1), 0)
    row = (position // NB * grid_rows + row_index) * NB + position % NB
    begin = offset + lax.broadcasted_iota(jnp.int32, (1, width), 1)
    return jnp.where(row < begin, 0.0, jnp.where(row == begin, 1.0, block))


def deal_kernel(in_ref, out_ref, *, pairs):
    lane = lax.broadcasted_iota(jnp.int32, (in_ref.shape[0], 128), 1)
    low = lane < NB
    for q in range(pairs):
        for t in range(4):
            a = in_ref[:, pl.ds(2 * q * 512 + t * 128, 128)]
            b = in_ref[:, pl.ds((2 * q + 1) * 512 + t * 128, 128)]
            out_ref[2 * t, :, pl.ds(q * 128, 128)] = jnp.where(low, a, pltpu.roll(b, NB, 1))
            out_ref[2 * t + 1, :, pl.ds(q * 128, 128)] = jnp.where(low, pltpu.roll(a, NB, 1), b)


def deal(vectors_t, grid_rows):
    narrow, total = vectors_t.shape
    local = total // grid_rows
    steps = 7
    return pl.pallas_call(
        lambda i, o: deal_kernel(i, o, pairs=local // 128 // steps),
        grid=(steps,),
        in_specs=[pl.BlockSpec((narrow, total // steps), lambda s: (0, s))],
        out_specs=pl.BlockSpec((grid_rows, narrow, local // steps), lambda s: (0, 0, s)),
        out_shape=jax.ShapeDtypeStruct((grid_rows, narrow, local), F32),
    )(vectors_t)


def inner_kernel(info, v_ref, r_ref, w_ref, o_ref, *, grid_rows):
    j = pl.program_id(0)
    rows = v_ref.shape[0]
    width = r_ref.shape[3]
    v_high, v_low = split(v_ref[...])
    both = jnp.concatenate([v_high, v_low], axis=1)
    narrow = v_ref.shape[1]

    @pl.when(j == 0)
    def _():
        o_ref[...] = w_ref[...]

    first = (info[3] * pl.num_programs(0) + j) * rows
    dims = (((0,), (0,)), ((), ()))
    for k in range(2):
        high, low = split(masked(r_ref[0, k], info[k], info[2], grid_rows, first))
        main = lax.dot_general(both, high, dims, preferred_element_type=F32)
        rest = lax.dot_general(v_high, low, dims, preferred_element_type=F32)
        o_ref[:, k * width : (k + 1) * width] += main[:narrow] + (main[narrow:] + rest)


def inner(info, v, gathered, start, grid_rows):
    count, panels, rows, width = gathered.shape
    narrow = v.shape[1]
    return pl.pallas_call(
        lambda *refs: inner_kernel(*refs, grid_rows=grid_rows),
        grid_spec=pltpu.PrefetchScalarGridSpec(
            num_scalar_prefetch=1,
            grid=(count,),
            in_specs=[
                pl.BlockSpec((rows, narrow), lambda j, s: (s[3] * count + j, 0)),
                pl.BlockSpec((1, panels, rows, width), lambda j, s: (j, 0, 0, 0)),
                pl.BlockSpec((narrow, panels * width), lambda j, s: (0, 0)),
            ],
            out_specs=pl.BlockSpec((narrow, panels * width), lambda j, s: (0, 0)),
        ),
        out_shape=jax.ShapeDtypeStruct((narrow, panels * width), F32),
        compiler_params=pltpu.CompilerParams(vmem_limit_bytes=48 * 1024 * 1024),
    )(info, v, gathered, start)


def solve_kernel(parts_ref, mix_ref, out_ref):
    total = parts_ref[0]
    for i in range(1, parts_ref.shape[0]):
        total += parts_ref[i]
    solved = jnp.dot(total, mix_ref[...], precision=lax.Precision.HIGHEST, preferred_element_type=F32)
    for i in range(parts_ref.shape[0]):
        out_ref[i] = solved


def solve(parts, mix):
    return pl.pallas_call(
        solve_kernel, out_shape=jax.ShapeDtypeStruct(parts.shape, F32)
    )(parts, mix)


def apply_kernel(info, v_ref, one_ref, two_ref, t_ref, o_ref, t_scr, *, grid_rows):
    h, j = pl.program_id(0), pl.program_id(1)
    rows, narrow = v_ref.shape
    width = one_ref.shape[3]

    @pl.when((h == 0) & (j == 0))
    def _():
        for k in range(2):
            high, low = split(t_ref[:, k * width : (k + 1) * width].T)
            t_scr[k, :, :narrow] = high
            t_scr[k, :, narrow:] = low

    half = jnp.where(h == 0, info[3], 1 - info[3])
    first = (half * pl.num_programs(1) + j) * rows

    def run(r_ref):
        total = v_ref[...]
        for k in range(2):
            high, low = split(masked(r_ref[0, k], info[k], info[2], grid_rows, first))
            main = jnp.dot(high, t_scr[k], preferred_element_type=F32)
            rest = jnp.dot(low, t_scr[k, :, :narrow], preferred_element_type=F32)
            total -= main[:, :narrow] + (main[:, narrow:] + rest)
        o_ref[...] = total

    @pl.when(h == 0)
    def _():
        run(one_ref)

    @pl.when(h == 1)
    def _():
        run(two_ref)


def apply(info, v, one, two, t, grid_rows):
    count, panels, rows, width = one.shape
    narrow = v.shape[1]

    def place(h, j, s):
        return (jnp.where(h == 0, s[3], 1 - s[3]) * count + j, 0)

    return pl.pallas_call(
        lambda *refs: apply_kernel(*refs, grid_rows=grid_rows),
        grid_spec=pltpu.PrefetchScalarGridSpec(
            num_scalar_prefetch=1,
            grid=(2, count),
            in_specs=[
                pl.BlockSpec((rows, narrow), place),
                pl.BlockSpec((1, panels, rows, width), lambda h, j, s: (jnp.where(h == 0, j, count - 1), 0, 0, 0)),
                pl.BlockSpec((1, panels, rows, width), lambda h, j, s: (jnp.where(h == 0, 0, j), 0, 0, 0)),
                pl.BlockSpec((narrow, panels * width), lambda h, j, s: (0, 0)),
            ],
            out_specs=pl.BlockSpec((rows, narrow), place),
            scratch_shapes=[pltpu.VMEM((panels, width, 2 * narrow), BF16)],
        ),
        out_shape=jax.ShapeDtypeStruct(v.shape, F32),
        compiler_params=pltpu.CompilerParams(vmem_limit_bytes=48 * 1024 * 1024),
    )(info, v, one, two, t)


def shards(vectors, panels, offsets, factor_upper, scales):
    grid_rows, grid_cols = lax.axis_size("row"), lax.axis_size("col")
    row_index, col_index = lax.axis_index("row"), lax.axis_index("col")
    everyone = grid_rows * grid_cols
    half = grid_cols // 2
    rows, width = panels.shape[1:]
    narrow = vectors.shape[1]
    groups = [list(range(half)), list(range(half, grid_cols))]
    side = col_index // half

    other = lax.ppermute(panels, "col", [(c, c ^ half) for c in range(grid_cols)])
    one = lax.all_gather(panels, "col", axis=0, axis_index_groups=groups)
    two = lax.all_gather(other, "col", axis=0, axis_index_groups=groups)

    reflect = [masked(panels[k], offsets[k], row_index, grid_rows, col_index * rows) for k in range(2)]
    gram = exact_dot(reflect[1].T, reflect[0])
    gram = lax.all_to_all(gram.reshape(everyone, width // everyone, width), ("row", "col"), 0, 0, tiled=True).sum(0)
    gram = lax.all_to_all(jnp.broadcast_to(gram[None], (everyone,) + gram.shape), ("row", "col"), 0, 0, tiled=True)
    gram = gram.reshape(width, width)
    factors = build_factors(factor_upper, scales)
    corner = exact_dot(factors[1], exact_dot(gram, factors[0]))
    mix = jnp.concatenate(
        [
            jnp.concatenate([factors[0].T, -corner.T], axis=1),
            jnp.concatenate([jnp.zeros((width, width), F32), factors[1].T], axis=1),
        ],
        axis=0,
    )

    dealt = deal(vectors.T, grid_rows)
    dealt, other = lax.optimization_barrier((dealt, other))
    moved = lax.all_to_all(dealt, "row", 0, 0, tiled=True)
    current = moved.reshape(grid_rows * narrow, -1).T

    def info(which):
        return jnp.stack([offsets[0], offsets[1], row_index.astype(jnp.int32), which.astype(jnp.int32)])

    start = jnp.zeros((grid_rows * narrow, 2 * width), F32)
    sums = inner(info(side), current, one, start, grid_rows)
    sums = inner(info(1 - side), current, two, sums, grid_rows)
    parts = lax.all_to_all(sums.reshape(grid_rows, narrow, 2 * width), "row", 0, 0, tiled=True)
    solved = solve(parts, mix)
    solved = lax.all_to_all(solved, "row", 0, 0, tiled=True).reshape(grid_rows * narrow, 2 * width)
    return apply(info(side), current, one, two, solved, grid_rows)


def solution(mesh):
    return jax.shard_map(
        shards,
        mesh=mesh,
        in_specs=(P(None, ("row", "col")), P(None, ("row", "col"), None), P(), P(), P()),
        out_specs=P("row", "col"),
        check_vma=False,
    )
```

```python
import jax
import jax.numpy as jnp
from jax import lax
from jax.experimental import pallas as pl
from jax.experimental.pallas import tpu as pltpu
from jax.sharding import PartitionSpec as P

NB = 64
F32 = jnp.float32
BF16 = jnp.bfloat16


def exact_dot(left, right):
    return jnp.dot(left, right, precision=lax.Precision.HIGHEST, preferred_element_type=F32)


def split(value):
    high = value.astype(BF16)
    return high, (value - high.astype(F32)).astype(BF16)


def masked(block, offset, row_index, grid_rows, first):
    rows, width = block.shape
    position = first + lax.broadcasted_iota(jnp.int32, (rows, 1), 0)
    row = (position // NB * grid_rows + row_index) * NB + position % NB
    begin = offset + lax.broadcasted_iota(jnp.int32, (1, width), 1)
    return jnp.where(row < begin, 0.0, jnp.where(row == begin, 1.0, block))


def deal_kernel(in_ref, out_ref, *, pairs):
    lane = lax.broadcasted_iota(jnp.int32, (in_ref.shape[0], 128), 1)
    low = lane < NB
    for q in range(pairs):
        for t in range(4):
            a = in_ref[:, pl.ds(2 * q * 512 + t * 128, 128)]
            b = in_ref[:, pl.ds((2 * q + 1) * 512 + t * 128, 128)]
            out_ref[2 * t, :, pl.ds(q * 128, 128)] = jnp.where(low, a, pltpu.roll(b, NB, 1))
            out_ref[2 * t + 1, :, pl.ds(q * 128, 128)] = jnp.where(low, pltpu.roll(a, NB, 1), b)


def deal(vectors_t, grid_rows):
    narrow, total = vectors_t.shape
    local = total // grid_rows
    steps = 7
    return pl.pallas_call(
        lambda i, o: deal_kernel(i, o, pairs=local // 128 // steps),
        grid=(steps,),
        in_specs=[pl.BlockSpec((narrow, total // steps), lambda s: (0, s))],
        out_specs=pl.BlockSpec((grid_rows, narrow, local // steps), lambda s: (0, 0, s)),
        out_shape=jax.ShapeDtypeStruct((grid_rows, narrow, local), F32),
    )(vectors_t)


def global_row(position, row_index, grid_rows):
    return (position // NB * grid_rows + row_index) * NB + position % NB


def start_block(info, views, held, sems, block, base, grid_rows):
    rows = views[0].shape[0]
    last = global_row(base + (block + 1) * rows - 1, info[2], grid_rows)
    for panel, view in enumerate(views):
        copy = pltpu.make_async_copy(
            view, held.at[panel, pl.ds(pl.multiple_of(block * rows, rows), rows)], sems.at[panel, block]
        )
        pl.when(last >= info[panel])(copy.start)


def wait_block(info, view, held, sems, block, base, grid_rows):
    rows = view.shape[0]
    last = global_row(base + (block + 1) * rows - 1, info[2], grid_rows)
    for panel in range(held.shape[0]):
        copy = pltpu.make_async_copy(
            view, held.at[panel, pl.ds(pl.multiple_of(block * rows, rows), rows)], sems.at[panel, block]
        )
        pl.when(last >= info[panel])(copy.wait)


def each_case(info, panel, first, rows, width, grid_rows, load, work):
    top = global_row(first, info[2], grid_rows)
    last = global_row(first + rows - 1, info[2], grid_rows)
    clear = top >= info[panel] + width

    @pl.when(clear)
    def _():
        work(load())

    @pl.when(jnp.logical_not(clear) & (last >= info[panel]))
    def _():
        work(masked(load(), info[panel], info[2], grid_rows, first))


def own_sources(ref):
    return [(j, [ref.at[j, k] for k in range(ref.shape[1])]) for j in range(ref.shape[0])]


def ring_block(info, step):
    return lax.rem(info[4] + step // 2, 4) * 2 + lax.rem(info[5] + step, 2)


def ring_sources(refs, info):
    near, near_across, *rest = refs
    views = [[whole.at[k] for k in range(2)] for whole in (near, near_across)]
    views += [[one, two] for one, two in zip(rest[::2], rest[1::2], strict=True)]
    return [(ring_block(info, step), pair) for step, pair in enumerate(views)]


def gram_kernel(info, r_ref, *refs, grid_rows):
    *o_refs, total = refs
    panels, rows, width = r_ref.shape
    first = info[3] * rows
    zero, one = [split(masked(r_ref[k], info[k], info[2], grid_rows, first)) for k in range(panels)]
    dims = (((0,), (0,)), ((), ()))

    def dot(left, right):
        return lax.dot_general(left, right, dims, preferred_element_type=F32)

    total[...] = dot(one[0], zero[0]) + (dot(one[0], zero[1]) + dot(one[1], zero[0]))
    part = width // len(o_refs)
    for step, o_ref in enumerate(o_refs):
        at = lax.rem(info[4] + step, len(o_refs)) * part
        o_ref[...] = total[pl.ds(pl.multiple_of(at, part), part), :]


def gram_parts(info, panels, parts, grid_rows):
    width = panels.shape[2]
    return pl.pallas_call(
        lambda *refs: gram_kernel(*refs, grid_rows=grid_rows),
        in_specs=[pl.BlockSpec(memory_space=pltpu.SMEM), pl.BlockSpec(memory_space=pltpu.VMEM)],
        out_specs=[pl.BlockSpec(memory_space=pltpu.VMEM)] * parts,
        out_shape=[jax.ShapeDtypeStruct((width // parts, width), F32)] * parts,
        scratch_shapes=[pltpu.VMEM((width, width), F32)],
        compiler_params=pltpu.CompilerParams(vmem_limit_bytes=16 * 1024 * 1024),
    )(info, panels)


def inner_kernel(info, v_ref, w_ref, *refs, count, grid_rows, chunk):
    *r_refs, o_ref, held, sems = refs
    narrow = v_ref.shape[0]
    panels, total, width = held.shape
    sources = own_sources(r_refs[0]) if len(r_refs) == 1 else ring_sources(r_refs, info)
    base = info[3] * total
    for block, views in sources:
        start_block(info, views, held, sems, block, base, grid_rows)
    o_ref[...] = w_ref[...]
    view = sources[0][1][0]
    wait_block(info, view, held, sems, 0, base, grid_rows)

    def step(q, carry):
        wait_block(info, view, held, sems, q + 1, base, grid_rows)
        at = pl.multiple_of(q * chunk, chunk)
        first = base + at
        for k in range(panels):

            def work(block, k=k):
                high, low = split(block)
                v_high, v_low = split(v_ref[:, pl.ds(pl.multiple_of(first, 128), chunk)])
                both = jnp.concatenate([v_high, v_low], axis=0)
                main = jnp.dot(both, high, preferred_element_type=F32)
                rest = jnp.dot(v_high, low, preferred_element_type=F32)
                o_ref[:, k * width : (k + 1) * width] += main[:narrow] + (main[narrow:] + rest)

            each_case(info, k, first, chunk, width, grid_rows, lambda k=k: held[k, pl.ds(at, chunk), :], work)
        return carry

    lax.fori_loop(0, count - 1, step, 0)


def inner(info, v, start, gathered, count, shape, grid_rows):
    panels, rows, width = shape
    narrow = v.shape[0]
    total = count * rows
    vmem = pl.BlockSpec(memory_space=pltpu.VMEM)
    return pl.pallas_call(
        lambda *refs: inner_kernel(*refs, count=count, grid_rows=grid_rows, chunk=total // (count - 1)),
        in_specs=[pl.BlockSpec(memory_space=pltpu.SMEM), vmem, vmem]
        + [pl.BlockSpec(memory_space=pltpu.HBM)] * len(gathered),
        out_specs=vmem,
        out_shape=jax.ShapeDtypeStruct((narrow, panels * width), F32),
        scratch_shapes=[
            pltpu.VMEM((panels, total, width), F32),
            pltpu.SemaphoreType.DMA((panels, count)),
        ],
        compiler_params=pltpu.CompilerParams(vmem_limit_bytes=50 * 1024 * 1024),
        cost_estimate=pl.CostEstimate(
            flops=6 * narrow * panels * total * width, bytes_accessed=4 * panels * total * width, transcendentals=0
        ),
    )(info, v, start, *gathered)


def solve_kernel(parts_ref, mix_ref, out_ref):
    total = parts_ref[0]
    for i in range(1, parts_ref.shape[0]):
        total += parts_ref[i]
    solved = jnp.dot(total, mix_ref[...], precision=lax.Precision.HIGHEST, preferred_element_type=F32)
    for i in range(parts_ref.shape[0]):
        out_ref[i] = solved


def solve(parts, mix):
    return pl.pallas_call(
        solve_kernel, out_shape=jax.ShapeDtypeStruct(parts.shape, F32)
    )(parts, mix)


def mixing_kernel(info, upper_ref, scales_ref, *refs):
    *part_refs, o_ref, gram = refs
    width = gram.shape[0]
    part = width // len(part_refs)
    for step, part_ref in enumerate(part_refs):
        at = lax.rem(info[3] + len(part_refs) - step, len(part_refs)) * part
        gram[pl.ds(pl.multiple_of(at, part), part), :] = part_ref[...]
    row = lax.broadcasted_iota(jnp.int32, (width, width), 0)
    column = lax.broadcasted_iota(jnp.int32, (width, width), 1)

    def factor(k):
        diagonal = jnp.where(row == column, scales_ref[k : k + 1, :], 0.0)
        return jnp.where(row < column, upper_ref[k], diagonal)

    zero, one = factor(0), factor(1)
    corner = exact_dot(one, exact_dot(gram[...], zero))
    o_ref[:width, :width] = zero.T
    o_ref[:width, width:] = -corner.T
    o_ref[width:, :width] = jnp.zeros((width, width), F32)
    o_ref[width:, width:] = one.T


def mixing(info, factor_upper, scales, parts):
    panels, width = scales.shape
    vmem = pl.BlockSpec(memory_space=pltpu.VMEM)
    return pl.pallas_call(
        mixing_kernel,
        in_specs=[pl.BlockSpec(memory_space=pltpu.SMEM)] + [vmem] * (2 + len(parts)),
        out_specs=vmem,
        out_shape=jax.ShapeDtypeStruct((panels * width, panels * width), F32),
        scratch_shapes=[pltpu.VMEM((width, width), F32)],
        compiler_params=pltpu.CompilerParams(vmem_limit_bytes=16 * 1024 * 1024),
    )(info, factor_upper, scales, *parts)


def apply_kernel(info, v_ref, t_ref, *refs, count, grid_rows):
    *r_refs, o_ref, t_scr, held, moving, sems, v_sems, o_sems = refs
    panels, total, width = held.shape
    narrow = t_ref.shape[0]
    rows = total // (2 * count)
    sources = [(info[3] * count + block, views) for block, views in own_sources(r_refs[0])]
    sources += [((1 - info[3]) * count + block, views) for block, views in ring_sources(r_refs[1:], info)]

    def place(block):
        return pl.ds(pl.multiple_of(block * rows, rows), rows)

    def v_copy(block):
        return pltpu.make_async_copy(v_ref.at[place(block)], moving.at[place(block)], v_sems.at[block])

    def o_copy(block):
        return pltpu.make_async_copy(moving.at[place(block)], o_ref.at[place(block)], o_sems.at[block])

    for block, views in sources:
        v_copy(block).start()
        start_block(info, views, held, sems, block, 0, grid_rows)
    for k in range(panels):
        high, low = split(t_ref[:, k * width : (k + 1) * width].T)
        t_scr[k, :, :narrow] = high
        t_scr[k, :, narrow:] = low

    def step(done, carry):
        far = (1 - info[3]) * count + ring_block(info, lax.max(done - count, 0))
        block = jnp.where(done < count, info[3] * count + done, far)
        first = block * rows
        v_copy(block).wait()
        wait_block(info, sources[0][1][0], held, sems, block, 0, grid_rows)
        for k in range(panels):

            def work(value, k=k):
                high, low = split(value)
                main = jnp.dot(high, t_scr[k], preferred_element_type=F32)
                rest = jnp.dot(low, t_scr[k, :, :narrow], preferred_element_type=F32)
                moving[place(block), :] -= main[:, :narrow] + (main[:, narrow:] + rest)

            each_case(info, k, first, rows, width, grid_rows, lambda k=k: held[k, place(block), :], work)
        o_copy(block).start()
        return carry

    lax.fori_loop(0, 2 * count, step, 0)
    for block in range(2 * count):
        o_copy(block).wait()


def apply(info, v, t, gathered, count, shape, grid_rows):
    panels, rows, width = shape
    narrow = v.shape[1]
    total = 2 * count * rows
    anywhere = pl.BlockSpec(memory_space=pltpu.HBM)
    return pl.pallas_call(
        lambda *refs: apply_kernel(*refs, count=count, grid_rows=grid_rows),
        in_specs=[pl.BlockSpec(memory_space=pltpu.SMEM), anywhere, pl.BlockSpec(memory_space=pltpu.VMEM)]
        + [anywhere] * len(gathered),
        out_specs=anywhere,
        out_shape=jax.ShapeDtypeStruct(v.shape, F32),
        scratch_shapes=[
            pltpu.VMEM((panels, width, 2 * narrow), BF16),
            pltpu.VMEM((panels, total, width), F32),
            pltpu.VMEM((total, narrow), F32),
            pltpu.SemaphoreType.DMA((panels, 2 * count)),
            pltpu.SemaphoreType.DMA((2 * count,)),
            pltpu.SemaphoreType.DMA((2 * count,)),
        ],
        compiler_params=pltpu.CompilerParams(vmem_limit_bytes=56 * 1024 * 1024),
        cost_estimate=pl.CostEstimate(
            flops=6 * narrow * panels * total * width, bytes_accessed=4 * panels * total * width, transcendentals=0
        ),
    )(info, v, t, *gathered)


def shards(vectors, panels, offsets, factor_upper, scales):
    grid_rows, grid_cols = lax.axis_size("row"), lax.axis_size("col")
    row_index, col_index = lax.axis_index("row"), lax.axis_index("col")
    half = grid_cols // 2
    rows, width = panels.shape[1:]
    narrow = vectors.shape[1]
    groups = [list(range(half)), list(range(half, grid_cols))]
    side, ring, core = col_index // half, col_index // 2 % 4, col_index % 2

    def along_col(value, to):
        return lax.ppermute(value, "col", [(c, to(c)) for c in range(grid_cols)])

    def along_row(value, to):
        return lax.ppermute(value, "row", [(r, to(r)) for r in range(grid_rows)])

    def up(c):
        return c // 8 * 8 + (c + 2) % 8

    def down(c):
        return c // 8 * 8 + (c + 6) % 8

    def across(value):
        return along_col(value, lambda c: c ^ 1)

    own = lax.all_gather(panels, "col", axis=0, axis_index_groups=groups)
    near = along_col(panels, lambda c: c ^ half)

    dealt = deal(vectors.T, grid_rows)
    level = row_index % 4

    def info(*ints):
        return jnp.stack([offsets[0], offsets[1]] + [i.astype(jnp.int32) for i in (row_index, *ints)])

    def others(value, move, steps):
        return sum([move(value, step) for step in steps], value)

    def shifted(step):
        return lambda r: r // 4 * 4 + (r + step) % 4

    gram, *parts = gram_parts(info(col_index, level), panels, 4, grid_rows)
    gram = others(gram, lambda _, step: along_row(parts[step - 1], shifted(step)), (1, 2, 3))
    gram = gram.reshape(2, width // 8, width)
    given = across(lax.dynamic_index_in_dim(gram, 1 - core, 0, False))
    gram = lax.dynamic_index_in_dim(gram, core, 0, False) + given
    gram = others(gram, lambda g, step: along_col(g, lambda c: c // 8 * 8 + (c + 2 * step) % 8), (1, 2, 3))
    every = [(r, c) for r in range(grid_rows) for c in range(grid_cols)]

    def along_x(value, step):
        flips = [((r ^ (step // 2 * 4)), (c ^ (step % 2 * 8))) for r, c in every]
        pairs = [(r * grid_cols + c, p * grid_cols + q) for (r, c), (p, q) in zip(every, flips, strict=True)]
        return lax.ppermute(value, ("row", "col"), pairs)

    gram = others(gram, along_x, (1, 2, 3))
    dealt, near, gram = lax.optimization_barrier((dealt, near, gram))

    moved = lax.all_to_all(dealt, "row", 0, 0, tiled=True).reshape(grid_rows * narrow, -1)
    parts = [near[k] for k in range(2)]
    below, above = [along_col(parts[k], up) for k in range(2)], [along_col(parts[k], down) for k in range(2)]
    near_across = across(near)
    given = across(gram)
    gram = jnp.where(core == 0, jnp.concatenate([gram, given]), jnp.concatenate([given, gram]))
    far = [along_col(below[0], up), along_col(above[1], down)]
    below_across, above_across = [across(part) for part in below], [across(part) for part in above]
    moved, near_across, gram = lax.optimization_barrier((moved, near_across, gram))
    far_across = [across(part) for part in far]
    ring_parts = [near, near_across, *above, *above_across, *far, *far_across, *below, *below_across]

    start = jnp.zeros((grid_rows * narrow, 2 * width), F32)
    sums = inner(info(side, ring, core), moved, start, [own], half, panels.shape, grid_rows)
    parts = [gram] + [along_row(gram, shifted(step)) for step in (1, 2, 3)]
    sums, *parts = lax.optimization_barrier((sums, *parts))
    mix = mixing(info(level), factor_upper, scales, parts)

    sums = inner(info(1 - side, ring, core), moved, sums, ring_parts, half, panels.shape, grid_rows)
    parts = lax.all_to_all(sums.reshape(grid_rows, narrow, 2 * width), "row", 0, 0, tiled=True)
    solved = solve(parts, mix)
    solved = lax.all_to_all(solved, "row", 0, 0, tiled=True).reshape(grid_rows * narrow, 2 * width)
    return apply(info(side, ring, core), moved.T, solved, [own] + ring_parts, half, panels.shape, grid_rows)


def solution(mesh):
    return jax.shard_map(
        shards,
        mesh=mesh,
        in_specs=(P(None, ("row", "col")), P(None, ("row", "col"), None), P(), P(), P()),
        out_specs=P("row", "col"),
        check_vma=False,
    )
```

```python
import jax
import jax.numpy as jnp
from jax import lax
from jax.experimental import pallas as pl
from jax.experimental.pallas import tpu as pltpu
from jax.sharding import PartitionSpec as P

NB = 64
F32 = jnp.float32
BF16 = jnp.bfloat16


def exact_dot(left, right):
    return jnp.dot(left, right, precision=lax.Precision.HIGHEST, preferred_element_type=F32)


def split(value):
    high = value.astype(BF16)
    return high, (value - high.astype(F32)).astype(BF16)


def masked(block, offset, row_index, grid_rows, first):
    rows, width = block.shape
    position = first + lax.broadcasted_iota(jnp.int32, (rows, 1), 0)
    row = (position // NB * grid_rows + row_index) * NB + position % NB
    begin = offset + lax.broadcasted_iota(jnp.int32, (1, width), 1)
    return jnp.where(row < begin, 0.0, jnp.where(row == begin, 1.0, block))


def deal_kernel(in_ref, out_ref, *, pairs):
    lane = lax.broadcasted_iota(jnp.int32, (in_ref.shape[0], 128), 1)
    low = lane < NB
    for q in range(pairs):
        for t in range(4):
            a = in_ref[:, pl.ds(2 * q * 512 + t * 128, 128)]
            b = in_ref[:, pl.ds((2 * q + 1) * 512 + t * 128, 128)]
            out_ref[2 * t, :, pl.ds(q * 128, 128)] = jnp.where(low, a, pltpu.roll(b, NB, 1))
            out_ref[2 * t + 1, :, pl.ds(q * 128, 128)] = jnp.where(low, pltpu.roll(a, NB, 1), b)


def deal(vectors_t, grid_rows):
    narrow, total = vectors_t.shape
    local = total // grid_rows
    steps = 7
    return pl.pallas_call(
        lambda i, o: deal_kernel(i, o, pairs=local // 128 // steps),
        grid=(steps,),
        in_specs=[pl.BlockSpec((narrow, total // steps), lambda s: (0, s))],
        out_specs=pl.BlockSpec((grid_rows, narrow, local // steps), lambda s: (0, 0, s)),
        out_shape=jax.ShapeDtypeStruct((grid_rows, narrow, local), F32),
    )(vectors_t)


def global_row(position, row_index, grid_rows):
    return (position // NB * grid_rows + row_index) * NB + position % NB


def start_block(info, views, held, sems, block, base, grid_rows):
    rows = views[0].shape[0]
    last = global_row(base + (block + 1) * rows - 1, info[2], grid_rows)
    for panel, view in enumerate(views):
        copy = pltpu.make_async_copy(
            view, held.at[panel, pl.ds(pl.multiple_of(block * rows, rows), rows)], sems.at[panel, block]
        )
        pl.when(last >= info[panel])(copy.start)


def wait_block(info, view, held, sems, block, base, grid_rows):
    rows = view.shape[0]
    last = global_row(base + (block + 1) * rows - 1, info[2], grid_rows)
    for panel in range(held.shape[0]):
        copy = pltpu.make_async_copy(
            view, held.at[panel, pl.ds(pl.multiple_of(block * rows, rows), rows)], sems.at[panel, block]
        )
        pl.when(last >= info[panel])(copy.wait)


def each_case(info, panel, first, rows, width, grid_rows, load, work):
    top = global_row(first, info[2], grid_rows)
    last = global_row(first + rows - 1, info[2], grid_rows)
    clear = top >= info[panel] + width

    @pl.when(clear)
    def _():
        work(load())

    @pl.when(jnp.logical_not(clear) & (last >= info[panel]))
    def _():
        work(masked(load(), info[panel], info[2], grid_rows, first))


def ring_block(info, step):
    return lax.rem(info[4] + step // 2, 4) * 2 + lax.rem(info[5] + step, 2)


def ring_sources(refs, info):
    return [(ring_block(info, step), [ref.at[k] for k in range(ref.shape[0])]) for step, ref in enumerate(refs)]


def gram_kernel(info, r_ref, *refs, grid_rows):
    *o_refs, total = refs
    panels, rows, width = r_ref.shape
    first = info[3] * rows
    zero, one = [split(masked(r_ref[k], info[k], info[2], grid_rows, first)) for k in range(panels)]
    dims = (((0,), (0,)), ((), ()))

    def dot(left, right):
        return lax.dot_general(left, right, dims, preferred_element_type=F32)

    total[...] = dot(one[0], zero[0]) + (dot(one[0], zero[1]) + dot(one[1], zero[0]))
    part = width // len(o_refs)
    for step, o_ref in enumerate(o_refs):
        at = lax.rem(info[4] + step, len(o_refs)) * part
        o_ref[...] = total[pl.ds(pl.multiple_of(at, part), part), :]


def gram_parts(info, panels, parts, grid_rows):
    width = panels.shape[2]
    return pl.pallas_call(
        lambda *refs: gram_kernel(*refs, grid_rows=grid_rows),
        in_specs=[pl.BlockSpec(memory_space=pltpu.SMEM), pl.BlockSpec(memory_space=pltpu.VMEM)],
        out_specs=[pl.BlockSpec(memory_space=pltpu.VMEM)] * parts,
        out_shape=[jax.ShapeDtypeStruct((width // parts, width), F32)] * parts,
        scratch_shapes=[pltpu.VMEM((width, width), F32)],
        compiler_params=pltpu.CompilerParams(vmem_limit_bytes=16 * 1024 * 1024),
    )(info, panels)


def inner_kernel(info, v_ref, w_ref, *refs, count, grid_rows, chunk):
    *r_refs, o_ref, held, sems = refs
    narrow = v_ref.shape[0]
    panels, total, width = held.shape
    sources = ring_sources(r_refs, info)
    base = info[3] * total
    for block, views in sources:
        start_block(info, views, held, sems, block, base, grid_rows)
    o_ref[...] = w_ref[...]
    view = sources[0][1][0]
    wait_block(info, view, held, sems, 0, base, grid_rows)

    def step(q, carry):
        wait_block(info, view, held, sems, q + 1, base, grid_rows)
        at = pl.multiple_of(q * chunk, chunk)
        first = base + at
        for k in range(panels):

            def work(block, k=k):
                high, low = split(block)
                v_high, v_low = split(v_ref[:, pl.ds(pl.multiple_of(first, 128), chunk)])
                both = jnp.concatenate([v_high, v_low], axis=0)
                main = jnp.dot(both, high, preferred_element_type=F32)
                rest = jnp.dot(v_high, low, preferred_element_type=F32)
                o_ref[:, k * width : (k + 1) * width] += main[:narrow] + (main[narrow:] + rest)

            each_case(info, k, first, chunk, width, grid_rows, lambda k=k: held[k, pl.ds(at, chunk), :], work)
        return carry

    lax.fori_loop(0, count - 1, step, 0)


def inner(info, v, start, gathered, count, shape, grid_rows):
    panels, rows, width = shape
    narrow = v.shape[0]
    total = count * rows
    vmem = pl.BlockSpec(memory_space=pltpu.VMEM)
    return pl.pallas_call(
        lambda *refs: inner_kernel(*refs, count=count, grid_rows=grid_rows, chunk=total // (count - 1)),
        in_specs=[pl.BlockSpec(memory_space=pltpu.SMEM), vmem, vmem]
        + [pl.BlockSpec(memory_space=pltpu.HBM)] * len(gathered),
        out_specs=vmem,
        out_shape=jax.ShapeDtypeStruct((narrow, panels * width), F32),
        scratch_shapes=[
            pltpu.VMEM((panels, total, width), F32),
            pltpu.SemaphoreType.DMA((panels, count)),
        ],
        compiler_params=pltpu.CompilerParams(vmem_limit_bytes=50 * 1024 * 1024),
        cost_estimate=pl.CostEstimate(
            flops=6 * narrow * panels * total * width, bytes_accessed=4 * panels * total * width, transcendentals=0
        ),
    )(info, v, start, *gathered)


def solve_kernel(parts_ref, mix_ref, out_ref):
    total = parts_ref[0]
    for i in range(1, parts_ref.shape[0]):
        total += parts_ref[i]
    solved = jnp.dot(total, mix_ref[...], precision=lax.Precision.HIGHEST, preferred_element_type=F32)
    for i in range(parts_ref.shape[0]):
        out_ref[i] = solved


def solve(parts, mix):
    return pl.pallas_call(
        solve_kernel, out_shape=jax.ShapeDtypeStruct(parts.shape, F32)
    )(parts, mix)


def mixing_kernel(upper_ref, scales_ref, gram_ref, o_ref):
    width = scales_ref.shape[1]
    gram = (gram_ref[:4] + gram_ref[4:]).reshape(width, width)
    row = lax.broadcasted_iota(jnp.int32, (width, width), 0)
    column = lax.broadcasted_iota(jnp.int32, (width, width), 1)

    def factor(k):
        diagonal = jnp.where(row == column, scales_ref[k : k + 1, :], 0.0)
        return jnp.where(row < column, upper_ref[k], diagonal)

    zero, one = factor(0), factor(1)
    corner = exact_dot(one, exact_dot(gram, zero))
    o_ref[:width, :width] = zero.T
    o_ref[:width, width:] = -corner.T
    o_ref[width:, :width] = jnp.zeros((width, width), F32)
    o_ref[width:, width:] = one.T


def mixing(factor_upper, scales, gram):
    panels, width = scales.shape
    return pl.pallas_call(
        mixing_kernel,
        out_shape=jax.ShapeDtypeStruct((panels * width, panels * width), F32),
        compiler_params=pltpu.CompilerParams(vmem_limit_bytes=16 * 1024 * 1024),
    )(factor_upper, scales, gram)


def apply_kernel(info, v_ref, t_ref, *refs, count, grid_rows):
    *r_refs, o_ref, t_scr, held, moving, sems, v_sems, o_sems = refs
    panels, total, width = held.shape
    narrow = t_ref.shape[0]
    rows = total // (2 * count)
    sources = [(info[3] * count + block, views) for block, views in ring_sources(r_refs[:count], info)]
    sources += [((1 - info[3]) * count + block, views) for block, views in ring_sources(r_refs[count:], info)]

    def place(block):
        return pl.ds(pl.multiple_of(block * rows, rows), rows)

    def v_copy(block):
        return pltpu.make_async_copy(v_ref.at[place(block)], moving.at[place(block)], v_sems.at[block])

    def o_copy(block):
        return pltpu.make_async_copy(moving.at[place(block)], o_ref.at[place(block)], o_sems.at[block])

    for block, views in sources:
        v_copy(block).start()
        start_block(info, views, held, sems, block, 0, grid_rows)
    for k in range(panels):
        high, low = split(t_ref[:, k * width : (k + 1) * width].T)
        t_scr[k, :, :narrow] = high
        t_scr[k, :, narrow:] = low

    def step(done, carry):
        half = jnp.where(done < count, info[3], 1 - info[3])
        block = half * count + ring_block(info, lax.rem(done, count))
        first = block * rows
        v_copy(block).wait()
        wait_block(info, sources[0][1][0], held, sems, block, 0, grid_rows)
        for k in range(panels):

            def work(value, k=k):
                high, low = split(value)
                main = jnp.dot(high, t_scr[k], preferred_element_type=F32)
                rest = jnp.dot(low, t_scr[k, :, :narrow], preferred_element_type=F32)
                moving[place(block), :] -= main[:, :narrow] + (main[:, narrow:] + rest)

            each_case(info, k, first, rows, width, grid_rows, lambda k=k: held[k, place(block), :], work)
        o_copy(block).start()
        return carry

    lax.fori_loop(0, 2 * count, step, 0)
    for block in range(2 * count):
        o_copy(block).wait()


def apply(info, v, t, gathered, count, shape, grid_rows):
    panels, rows, width = shape
    narrow = v.shape[1]
    total = 2 * count * rows
    anywhere = pl.BlockSpec(memory_space=pltpu.HBM)
    return pl.pallas_call(
        lambda *refs: apply_kernel(*refs, count=count, grid_rows=grid_rows),
        in_specs=[pl.BlockSpec(memory_space=pltpu.SMEM), anywhere, pl.BlockSpec(memory_space=pltpu.VMEM)]
        + [anywhere] * len(gathered),
        out_specs=anywhere,
        out_shape=jax.ShapeDtypeStruct(v.shape, F32),
        scratch_shapes=[
            pltpu.VMEM((panels, width, 2 * narrow), BF16),
            pltpu.VMEM((panels, total, width), F32),
            pltpu.VMEM((total, narrow), F32),
            pltpu.SemaphoreType.DMA((panels, 2 * count)),
            pltpu.SemaphoreType.DMA((2 * count,)),
            pltpu.SemaphoreType.DMA((2 * count,)),
        ],
        compiler_params=pltpu.CompilerParams(vmem_limit_bytes=56 * 1024 * 1024),
        cost_estimate=pl.CostEstimate(
            flops=6 * narrow * panels * total * width, bytes_accessed=4 * panels * total * width, transcendentals=0
        ),
    )(info, v, t, *gathered)


def shards(vectors, panels, offsets, factor_upper, scales):
    grid_rows, grid_cols = lax.axis_size("row"), lax.axis_size("col")
    row_index, col_index = lax.axis_index("row"), lax.axis_index("col")
    half = grid_cols // 2
    rows, width = panels.shape[1:]
    narrow = vectors.shape[1]
    side, ring, core = col_index // half, col_index // 2 % 4, col_index % 2

    def along_col(value, to):
        return lax.ppermute(value, "col", [(c, to(c)) for c in range(grid_cols)])

    def along_row(value, to):
        return lax.ppermute(value, "row", [(r, to(r)) for r in range(grid_rows)])

    def up(c):
        return c // 8 * 8 + (c + 2) % 8

    def down(c):
        return c // 8 * 8 + (c + 6) % 8

    def across(value):
        return along_col(value, lambda c: c ^ 1)

    def info(*ints):
        return jnp.stack([offsets[0], offsets[1]] + [i.astype(jnp.int32) for i in (row_index, *ints)])

    def shifted(step):
        return lambda r: r // 4 * 4 + (r + step) % 4

    def turned(step):
        return lambda c: c // 8 * 8 + (c + 2 * step) % 8

    below, above = along_col(panels, up), along_col(panels, down)
    near = along_col(panels, lambda c: c ^ half)
    panels_across = across(panels)

    dealt = deal(vectors.T, grid_rows)
    level = row_index % 4
    gram, *parts = gram_parts(info(col_index, level), panels, 4, grid_rows)
    gram = sum([along_row(parts[step - 1], shifted(step)) for step in (1, 2, 3)], gram)
    gram = gram.reshape(2, width // 8, width)
    given = across(lax.dynamic_index_in_dim(gram, 1 - core, 0, False))
    gram = lax.dynamic_index_in_dim(gram, core, 0, False) + given
    gram = gram + along_col(gram, lambda c: c ^ half)
    below, above, near, dealt, gram, panels_across = lax.optimization_barrier(
        (below, above, near, dealt, gram, panels_across)
    )

    far = along_col(below, up)
    other_above = along_col(near, down)
    moved = lax.all_to_all(dealt, "row", 0, 0, tiled=True).reshape(grid_rows * narrow, -1)
    crossed = [across(below), across(above), across(near)]
    gram, *crossed = lax.optimization_barrier((gram, *crossed))
    below_across, above_across, near_across = crossed
    gram = sum([along_col(gram, turned(step)) for step in (1, 2, 3)], gram)
    other_above, far, near, gram = lax.optimization_barrier((other_above, far, near, gram))

    other_below, other_far = along_col(near, up), along_col(other_above, down)
    other_above_across, far_across = across(other_above), across(far)
    given = across(gram)
    gram = jnp.where(core == 0, jnp.concatenate([gram, given]), jnp.concatenate([given, gram]))
    moved, gram, other_above_across, far_across = lax.optimization_barrier(
        (moved, gram, other_above_across, far_across)
    )

    own = [panels, panels_across, above, above_across, far, far_across, below, below_across]
    start = jnp.zeros((grid_rows * narrow, 2 * width), F32)
    sums = inner(info(side, ring, core), moved, start, own, half, panels.shape, grid_rows)
    sums, gram, other_far, other_below = lax.optimization_barrier((sums, gram, other_far, other_below))
    other = [near, near_across, other_above, other_above_across]
    other += [other_far, across(other_far), other_below, across(other_below)]
    gram = jnp.broadcast_to(gram[None], (grid_rows,) + gram.shape)
    gram = lax.all_to_all(gram, "row", 0, 0, tiled=True)
    mix = mixing(factor_upper, scales, gram)

    sums = inner(info(1 - side, ring, core), moved, sums, other, half, panels.shape, grid_rows)
    parts = lax.all_to_all(sums.reshape(grid_rows, narrow, 2 * width), "row", 0, 0, tiled=True)
    solved = solve(parts, mix)
    solved = lax.all_to_all(solved, "row", 0, 0, tiled=True).reshape(grid_rows * narrow, 2 * width)
    return apply(info(side, ring, core), moved.T, solved, own + other, half, panels.shape, grid_rows)


def solution(mesh):
    return jax.shard_map(
        shards,
        mesh=mesh,
        in_specs=(P(None, ("row", "col")), P(None, ("row", "col"), None), P(), P(), P()),
        out_specs=P("row", "col"),
        check_vma=False,
    )
```

```python
import jax
import jax.numpy as jnp
from jax import lax
from jax.experimental import pallas as pl
from jax.experimental.pallas import tpu as pltpu
from jax.sharding import PartitionSpec as P

NB = 64
F32 = jnp.float32
BF16 = jnp.bfloat16


def exact_dot(left, right):
    return jnp.dot(left, right, precision=lax.Precision.HIGHEST, preferred_element_type=F32)


def split(value):
    high = value.astype(BF16)
    return high, (value - high.astype(F32)).astype(BF16)


def masked(block, offset, row_index, grid_rows, first):
    rows, width = block.shape
    position = first + lax.broadcasted_iota(jnp.int32, (rows, 1), 0)
    row = (position // NB * grid_rows + row_index) * NB + position % NB
    begin = offset + lax.broadcasted_iota(jnp.int32, (1, width), 1)
    return jnp.where(row < begin, 0.0, jnp.where(row == begin, 1.0, block))


def deal_kernel(in_ref, out_ref, *, pairs):
    lane = lax.broadcasted_iota(jnp.int32, (in_ref.shape[0], 128), 1)
    low = lane < NB
    for q in range(pairs):
        for t in range(4):
            a = in_ref[:, pl.ds(2 * q * 512 + t * 128, 128)]
            b = in_ref[:, pl.ds((2 * q + 1) * 512 + t * 128, 128)]
            out_ref[2 * t, :, pl.ds(q * 128, 128)] = jnp.where(low, a, pltpu.roll(b, NB, 1))
            out_ref[2 * t + 1, :, pl.ds(q * 128, 128)] = jnp.where(low, pltpu.roll(a, NB, 1), b)


def deal(vectors_t, grid_rows):
    narrow, total = vectors_t.shape
    local = total // grid_rows
    steps = 7
    return pl.pallas_call(
        lambda i, o: deal_kernel(i, o, pairs=local // 128 // steps),
        grid=(steps,),
        in_specs=[pl.BlockSpec((narrow, total // steps), lambda s: (0, s))],
        out_specs=pl.BlockSpec((grid_rows, narrow, local // steps), lambda s: (0, 0, s)),
        out_shape=jax.ShapeDtypeStruct((grid_rows, narrow, local), F32),
    )(vectors_t)


def global_row(position, row_index, grid_rows):
    return (position // NB * grid_rows + row_index) * NB + position % NB


def start_block(info, views, held, sems, block, base, grid_rows):
    rows = views[0].shape[0]
    last = global_row(base + (block + 1) * rows - 1, info[2], grid_rows)
    for panel, view in enumerate(views):
        copy = pltpu.make_async_copy(
            view, held.at[panel, pl.ds(pl.multiple_of(block * rows, rows), rows)], sems.at[panel, block]
        )
        pl.when(last >= info[panel])(copy.start)


def wait_block(info, view, held, sems, block, base, grid_rows):
    rows = view.shape[0]
    last = global_row(base + (block + 1) * rows - 1, info[2], grid_rows)
    for panel in range(held.shape[0]):
        copy = pltpu.make_async_copy(
            view, held.at[panel, pl.ds(pl.multiple_of(block * rows, rows), rows)], sems.at[panel, block]
        )
        pl.when(last >= info[panel])(copy.wait)


def each_case(info, panel, first, rows, width, grid_rows, load, work):
    top = global_row(first, info[2], grid_rows)
    last = global_row(first + rows - 1, info[2], grid_rows)
    clear = top >= info[panel] + width

    @pl.when(clear)
    def _():
        work(load())

    @pl.when(jnp.logical_not(clear) & (last >= info[panel]))
    def _():
        work(masked(load(), info[panel], info[2], grid_rows, first))


def ring_block(info, step):
    return lax.rem(info[4] + step // 2, 4) * 2 + lax.rem(info[5] + step, 2)


def ring_sources(refs, info):
    return [(ring_block(info, step), [ref.at[k] for k in range(ref.shape[0])]) for step, ref in enumerate(refs)]


def gram_kernel(info, r_ref, *refs, grid_rows):
    *o_refs, total = refs
    panels, rows, width = r_ref.shape
    first = info[3] * rows
    zero, one = [split(masked(r_ref[k], info[k], info[2], grid_rows, first)) for k in range(panels)]
    dims = (((0,), (0,)), ((), ()))

    def dot(left, right):
        return lax.dot_general(left, right, dims, preferred_element_type=F32)

    total[...] = dot(one[0], zero[0]) + (dot(one[0], zero[1]) + dot(one[1], zero[0]))
    part = width // len(o_refs)
    for step, o_ref in enumerate(o_refs):
        at = lax.rem(info[4] + step, len(o_refs)) * part
        o_ref[...] = total[pl.ds(pl.multiple_of(at, part), part), :]


def gram_parts(info, panels, parts, grid_rows):
    width = panels.shape[2]
    return pl.pallas_call(
        lambda *refs: gram_kernel(*refs, grid_rows=grid_rows),
        in_specs=[pl.BlockSpec(memory_space=pltpu.SMEM), pl.BlockSpec(memory_space=pltpu.VMEM)],
        out_specs=[pl.BlockSpec(memory_space=pltpu.VMEM)] * parts,
        out_shape=[jax.ShapeDtypeStruct((width // parts, width), F32)] * parts,
        scratch_shapes=[pltpu.VMEM((width, width), F32)],
        compiler_params=pltpu.CompilerParams(vmem_limit_bytes=16 * 1024 * 1024),
    )(info, panels)


def inner_kernel(info, v_ref, w_ref, *refs, count, parts, grid_rows, chunk):
    r_refs, refs = refs[:count], refs[count:]
    o_refs, (high_ref, low_ref, held, v_held, total, sems, v_sems) = refs[:parts], refs[parts:]
    narrow = v_ref.shape[0]
    panels, depth, width = held.shape
    sources = ring_sources(r_refs, info)
    base = info[3] * depth

    def v_copy(q):
        from_at = pl.ds(pl.multiple_of(base + q * chunk, 128), chunk)
        to_at = pl.ds(pl.multiple_of(q * chunk, 128), chunk)
        return pltpu.make_async_copy(v_ref.at[:, from_at], v_held.at[:, to_at], v_sems.at[q])

    for turn_at, (block, views) in enumerate(sources):
        if turn_at < count - 1:
            v_copy(lax.rem(2 * info[4] + turn_at, count - 1)).start()
        start_block(info, views, held, sems, block, base, grid_rows)
    total[...] = w_ref[...]
    view = sources[0][1][0]
    begin = 2 * info[4]

    def step(done, carry):
        turn_at, k = done // panels, lax.rem(done, panels)
        q = lax.rem(begin + turn_at, count - 1)
        at = pl.multiple_of(q * chunk, chunk)
        first = base + at
        across = pl.ds(pl.multiple_of(k * width, width), width)

        pl.when(k == 0)(v_copy(q).wait)

        @pl.when((k == 0) & ((q == 0) | (turn_at == 0)))
        def _():
            wait_block(info, view, held, sems, q, base, grid_rows)

        @pl.when((k == 0) & (q + 1 != begin))
        def _():
            wait_block(info, view, held, sems, q + 1, base, grid_rows)

        def work(block):
            high, low = split(block)
            high_ref[pl.ds(at, chunk), across] = high
            low_ref[pl.ds(at, chunk), across] = low
            v_high, v_low = split(v_held[:, pl.ds(pl.multiple_of(q * chunk, 128), chunk)])
            both = jnp.concatenate([v_high, v_low], axis=0)
            main = jnp.dot(both, high, preferred_element_type=F32)
            rest = jnp.dot(v_high, low, preferred_element_type=F32)
            total[:, across] += main[:narrow] + (main[narrow:] + rest)

        each_case(info, k, first, chunk, width, grid_rows, lambda: held[k, pl.ds(at, chunk), :], work)
        return carry

    lax.fori_loop(0, (count - 1) * panels, step, 0)
    size = narrow // parts
    for part, o_ref in enumerate(o_refs):
        at = lax.rem(info[6] + part, parts) * size
        o_ref[...] = total[pl.ds(pl.multiple_of(at, size), size), :]


def inner(info, v, start, gathered, parts, shape, grid_rows):
    panels, rows, width = shape
    narrow = v.shape[0]
    count = len(gathered)
    total = count * rows
    vmem = pl.BlockSpec(memory_space=pltpu.VMEM)
    *sums, high, low = pl.pallas_call(
        lambda *refs: inner_kernel(
            *refs, count=count, parts=parts, grid_rows=grid_rows, chunk=total // (count - 1)
        ),
        in_specs=[pl.BlockSpec(memory_space=pltpu.SMEM), pl.BlockSpec(memory_space=pltpu.HBM), vmem]
        + [pl.BlockSpec(memory_space=pltpu.HBM)] * count,
        out_specs=[vmem] * (parts + 2),
        out_shape=[jax.ShapeDtypeStruct((narrow // parts, panels * width), F32)] * parts
        + [jax.ShapeDtypeStruct((total, panels * width), BF16)] * 2,
        scratch_shapes=[
            pltpu.VMEM((panels, total, width), F32),
            pltpu.VMEM((narrow, total), F32),
            pltpu.VMEM((narrow, panels * width), F32),
            pltpu.SemaphoreType.DMA((panels, count)),
            pltpu.SemaphoreType.DMA((count - 1,)),
        ],
        compiler_params=pltpu.CompilerParams(vmem_limit_bytes=22 * 1024 * 1024),
        cost_estimate=pl.CostEstimate(
            flops=6 * narrow * panels * total * width, bytes_accessed=4 * panels * total * width, transcendentals=0
        ),
    )(info, v, start, *gathered)
    return sums, (high, low)


def add_kernel(*refs):
    *parts, o_ref = refs
    total = parts[0][...]
    for part in parts[1:]:
        total += part[...]
    o_ref[...] = total


def add(*parts):
    return pl.pallas_call(
        add_kernel,
        out_shape=jax.ShapeDtypeStruct(parts[0].shape, F32),
        compiler_params=pltpu.CompilerParams(vmem_limit_bytes=2 * 1024 * 1024),
    )(*parts)


def solve_kernel(mine_ref, given_ref, mix_ref, out_ref):
    out_ref[...] = exact_dot(mine_ref[...] + given_ref[...], mix_ref[...])


def solve(mine, given, mix):
    return pl.pallas_call(
        solve_kernel,
        out_shape=jax.ShapeDtypeStruct(mine.shape, F32),
        compiler_params=pltpu.CompilerParams(vmem_limit_bytes=4 * 1024 * 1024),
    )(mine, given, mix)


def turn_kernel(v_ref, o_ref, held, sems, *, chunk):
    steps = o_ref.shape[0] // chunk

    def copy(q):
        at = pl.ds(pl.multiple_of(q * chunk, chunk), chunk)
        return pltpu.make_async_copy(v_ref.at[:, at], held.at[:, at], sems.at[q])

    for q in range(steps):
        copy(q).start()

    def step(q, carry):
        copy(q).wait()
        at = pl.ds(pl.multiple_of(q * chunk, chunk), chunk)
        o_ref[at, :] = held[:, at].T
        return carry

    lax.fori_loop(0, steps, step, 0)


def turn(v, chunk):
    return pl.pallas_call(
        lambda *refs: turn_kernel(*refs, chunk=chunk),
        in_specs=[pl.BlockSpec(memory_space=pltpu.HBM)],
        out_specs=pl.BlockSpec(memory_space=pltpu.VMEM),
        out_shape=jax.ShapeDtypeStruct(v.shape[::-1], F32),
        scratch_shapes=[pltpu.VMEM(v.shape, F32), pltpu.SemaphoreType.DMA((v.shape[1] // chunk,))],
        compiler_params=pltpu.CompilerParams(vmem_limit_bytes=9 * 1024 * 1024),
    )(v)


def mixing_kernel(info, upper_ref, scales_ref, *refs):
    *part_refs, o_ref, gram = refs
    width = gram.shape[0]
    part = width // len(part_refs)
    for step, part_ref in enumerate(part_refs):
        at = lax.rem(info[6] + len(part_refs) - step, len(part_refs)) * part
        gram[pl.ds(pl.multiple_of(at, part), part), :] = part_ref[...]
    row = lax.broadcasted_iota(jnp.int32, (width, width), 0)
    column = lax.broadcasted_iota(jnp.int32, (width, width), 1)

    def factor(k):
        diagonal = jnp.where(row == column, scales_ref[k : k + 1, :], 0.0)
        return jnp.where(row < column, upper_ref[k], diagonal)

    zero, one = factor(0), factor(1)
    corner = exact_dot(one, exact_dot(gram[...], zero))
    o_ref[:width, :width] = zero.T
    o_ref[:width, width:] = -corner.T
    o_ref[width:, :width] = jnp.zeros((width, width), F32)
    o_ref[width:, width:] = one.T


def mixing(info, factor_upper, scales, parts):
    panels, width = scales.shape
    vmem = pl.BlockSpec(memory_space=pltpu.VMEM)
    return pl.pallas_call(
        mixing_kernel,
        in_specs=[pl.BlockSpec(memory_space=pltpu.SMEM)] + [vmem] * (2 + len(parts)),
        out_specs=vmem,
        out_shape=jax.ShapeDtypeStruct((panels * width, panels * width), F32),
        scratch_shapes=[pltpu.VMEM((width, width), F32)],
        compiler_params=pltpu.CompilerParams(vmem_limit_bytes=8 * 1024 * 1024),
    )(info, factor_upper, scales, *parts)


def apply_kernel(info, v_ref, *refs, parts, chunk, grid_rows):
    t_refs, refs = refs[:parts], refs[parts:]
    halves, (o_ref, t_all, t_scr, held, sems) = refs[:4], refs[4:]
    total, depth = halves[0].shape
    panels, width, _ = t_scr.shape
    size = t_refs[0].shape[0]
    narrow = size * parts
    for part, t_ref in enumerate(t_refs):
        at = lax.rem(info[6] + parts - part, parts) * size
        t_all[pl.ds(pl.multiple_of(at, size), size), :] = t_ref[...]
    for k in range(panels):
        high, low = split(t_all[:, k * width : (k + 1) * width].T)
        t_scr[k, :, :narrow] = high
        t_scr[k, :, narrow:] = low
    steps, slots = total // chunk, held.shape[0]

    def copy_of(slot, first):
        return pltpu.make_async_copy(held.at[slot], o_ref.at[pl.ds(first, chunk), :], sems.at[slot])

    for half, (high_ref, low_ref) in enumerate((halves[:2], halves[2:])):
        side = info[3] if half == 0 else 1 - info[3]

        def step(q, carry, half=half, side=side, high_ref=high_ref, low_ref=low_ref):
            at = pl.multiple_of(q * chunk, chunk)
            first = pl.multiple_of(side * total + at, chunk)
            done = half * steps + q
            slot = lax.rem(done, slots)
            pl.when(done >= slots)(copy_of(slot, first).wait)
            held[slot] = v_ref[pl.ds(first, chunk), :]
            last = global_row(first + chunk - 1, info[2], grid_rows)

            def panel(k, carry):
                across = pl.ds(pl.multiple_of(k * width, width), width)

                @pl.when(last >= info[k])
                def _():
                    main = jnp.dot(high_ref[pl.ds(at, chunk), across], t_scr[k], preferred_element_type=F32)
                    rest = jnp.dot(
                        low_ref[pl.ds(at, chunk), across], t_scr[k, :, :narrow], preferred_element_type=F32
                    )
                    held[slot] -= main[:, :narrow] + (main[:, narrow:] + rest)

                return carry

            lax.fori_loop(0, panels, panel, 0)
            copy_of(slot, first).start()
            return carry

        lax.fori_loop(0, steps, step, 0)
    for slot in range(slots):
        copy_of(slot, 0).wait()


def apply(info, v, t, own, other, chunk, grid_rows):
    narrow = v.shape[1]
    depth = t[0].shape[1]
    slots = 7
    vmem = pl.BlockSpec(memory_space=pltpu.VMEM)
    return pl.pallas_call(
        lambda *refs: apply_kernel(*refs, parts=len(t), chunk=chunk, grid_rows=grid_rows),
        in_specs=[pl.BlockSpec(memory_space=pltpu.SMEM)] + [vmem] * (5 + len(t)),
        out_specs=pl.BlockSpec(memory_space=pltpu.HBM),
        out_shape=jax.ShapeDtypeStruct(v.shape, F32),
        scratch_shapes=[
            pltpu.VMEM((narrow, depth), F32),
            pltpu.VMEM((2, depth // 2, 2 * narrow), BF16),
            pltpu.VMEM((slots, chunk, narrow), F32),
            pltpu.SemaphoreType.DMA((slots,)),
        ],
        compiler_params=pltpu.CompilerParams(vmem_limit_bytes=10 * 1024 * 1024),
    )(info, v, *t, *own, *other)


def shards(vectors, panels, offsets, factor_upper, scales):
    grid_rows, grid_cols = lax.axis_size("row"), lax.axis_size("col")
    row_index, col_index = lax.axis_index("row"), lax.axis_index("col")
    half = grid_cols // 2
    rows, width = panels.shape[1:]
    narrow = vectors.shape[1]
    side, ring, core = col_index // half, col_index // 2 % 4, col_index % 2

    def along_col(value, to):
        return lax.ppermute(value, "col", [(c, to(c)) for c in range(grid_cols)])

    def along_row(value, to):
        return lax.ppermute(value, "row", [(r, to(r)) for r in range(grid_rows)])

    def up(c):
        return c // 8 * 8 + (c + 2) % 8

    def down(c):
        return c // 8 * 8 + (c + 6) % 8

    def across(value):
        return along_col(value, lambda c: c ^ 1)

    def info(*ints):
        return jnp.stack([offsets[0], offsets[1]] + [i.astype(jnp.int32) for i in (row_index, *ints)])

    def shifted(step):
        return lambda r: r // 4 * 4 + (r + step) % 4

    def turned(step):
        return lambda c: c // 8 * 8 + (c + 2 * step) % 8

    below, above = along_col(panels, up), along_col(panels, down)
    near = along_col(panels, lambda c: c ^ half)
    panels_across = across(panels)

    dealt = deal(vectors.T, grid_rows)
    level = row_index % 4
    gram, *parts = gram_parts(info(col_index, level), panels, 4, grid_rows)
    gram = sum([along_row(parts[step - 1], shifted(step)) for step in (1, 2, 3)], gram)
    gram = gram.reshape(2, width // 8, width)
    given = across(lax.dynamic_index_in_dim(gram, 1 - core, 0, False))
    gram = lax.dynamic_index_in_dim(gram, core, 0, False) + given
    gram = gram + along_col(gram, lambda c: c ^ half)
    below, above, near, dealt, gram, panels_across = lax.optimization_barrier(
        (below, above, near, dealt, gram, panels_across)
    )

    far = along_col(below, up)
    other_above = along_col(near, down)
    moved = lax.all_to_all(dealt, "row", 0, 0, tiled=True).reshape(grid_rows * narrow, -1)
    crossed = [across(below), across(above), across(near)]
    gram, *crossed = lax.optimization_barrier((gram, *crossed))
    below_across, above_across, near_across = crossed
    gram = sum([along_col(gram, turned(step)) for step in (1, 2, 3)], gram)
    other_above, far, near, gram = lax.optimization_barrier((other_above, far, near, gram))

    other_below, other_far = along_col(near, up), along_col(other_above, down)
    other_above_across, far_across = across(other_above), across(far)
    given = across(gram)
    gram = jnp.where(core == 0, jnp.concatenate([gram, given]), jnp.concatenate([given, gram]))
    gram = gram + along_row(gram, lambda r: r ^ 4)
    own_info, other_info = info(side, ring, core, level), info(1 - side, ring, core, level)
    moved, gram, other_above_across, far_across, own_info, other_info = lax.optimization_barrier(
        (moved, gram, other_above_across, far_across, own_info, other_info)
    )

    moved = pltpu.with_memory_space_constraint(moved, pltpu.HBM)

    chunk = half * rows // (half - 1)
    own = [panels, panels_across, above, above_across, far, far_across, below, below_across]
    own = [pltpu.with_memory_space_constraint(part, pltpu.HBM) for part in own]
    start = jnp.zeros((grid_rows * narrow, 2 * width), F32)
    grams = [gram] + [along_row(gram, shifted(step)) for step in (1, 2, 3)]
    sums, own = inner(own_info, moved, start, own, 1, panels.shape, grid_rows)
    sums, other_far, other_below, *grams = lax.optimization_barrier((*sums, other_far, other_below, *grams))
    other = [near, near_across, other_above, other_above_across, other_far, other_below]
    other = [pltpu.with_memory_space_constraint(part, pltpu.HBM) for part in other]
    other[5:] = [across(other_far), other[5], across(other_below)]
    sums, current = lax.optimization_barrier((sums, turn(moved, 896)))
    (mine, *sums), other = inner(other_info, moved, sums, other, 4, panels.shape, grid_rows)

    mine = add(mine, *[along_row(sums[step - 1], shifted(step)) for step in (1, 2, 3)])
    mix = mixing(own_info, factor_upper, scales, grams)
    solved = solve(mine, along_row(mine, lambda r: r ^ 4), mix)
    solved = [solved] + [along_row(solved, shifted(step)) for step in (1, 2, 3)]
    return apply(own_info, current, solved, own, other, chunk, grid_rows)


def solution(mesh):
    return jax.shard_map(
        shards,
        mesh=mesh,
        in_specs=(P(None, ("row", "col")), P(None, ("row", "col"), None), P(), P(), P()),
        out_specs=P("row", "col"),
        check_vma=False,
    )
```

```python
import jax
import jax.numpy as jnp
from jax import lax
from jax.experimental import pallas as pl
from jax.experimental.pallas import tpu as pltpu
from jax.sharding import PartitionSpec as P

NB = 64
F32 = jnp.float32
BF16 = jnp.bfloat16


def exact_dot(left, right):
    return jnp.dot(left, right, precision=lax.Precision.HIGHEST, preferred_element_type=F32)


def split(value):
    high = value.astype(BF16)
    return high, (value - high.astype(F32)).astype(BF16)


def masked(block, offset, row_index, grid_rows, first):
    rows, width = block.shape
    position = first + lax.broadcasted_iota(jnp.int32, (rows, 1), 0)
    row = (position // NB * grid_rows + row_index) * NB + position % NB
    begin = offset + lax.broadcasted_iota(jnp.int32, (1, width), 1)
    return jnp.where(row < begin, 0.0, jnp.where(row == begin, 1.0, block))


def deal_kernel(in_ref, out_ref, *, pairs):
    lane = lax.broadcasted_iota(jnp.int32, (in_ref.shape[0], 128), 1)
    low = lane < NB
    for q in range(pairs):
        for t in range(4):
            a = in_ref[:, pl.ds(2 * q * 512 + t * 128, 128)]
            b = in_ref[:, pl.ds((2 * q + 1) * 512 + t * 128, 128)]
            out_ref[2 * t, :, pl.ds(q * 128, 128)] = jnp.where(low, a, pltpu.roll(b, NB, 1))
            out_ref[2 * t + 1, :, pl.ds(q * 128, 128)] = jnp.where(low, pltpu.roll(a, NB, 1), b)


def deal(vectors_t, grid_rows):
    narrow, total = vectors_t.shape
    local = total // grid_rows
    steps = 7
    return pl.pallas_call(
        lambda i, o: deal_kernel(i, o, pairs=local // 128 // steps),
        grid=(steps,),
        in_specs=[pl.BlockSpec((narrow, total // steps), lambda s: (0, s))],
        out_specs=pl.BlockSpec((grid_rows, narrow, local // steps), lambda s: (0, 0, s)),
        out_shape=jax.ShapeDtypeStruct((grid_rows, narrow, local), F32),
    )(vectors_t)


def global_row(position, row_index, grid_rows):
    return (position // NB * grid_rows + row_index) * NB + position % NB


def start_block(info, views, held, sems, block, base, grid_rows):
    rows = views[0].shape[0]
    last = global_row(base + (block + 1) * rows - 1, info[2], grid_rows)
    for panel, view in enumerate(views):
        copy = pltpu.make_async_copy(
            view, held.at[panel, pl.ds(pl.multiple_of(block * rows, rows), rows)], sems.at[panel, block]
        )
        pl.when(last >= info[panel])(copy.start)


def wait_block(info, view, held, sems, block, base, grid_rows):
    rows = view.shape[0]
    last = global_row(base + (block + 1) * rows - 1, info[2], grid_rows)
    for panel in range(held.shape[0]):
        copy = pltpu.make_async_copy(
            view, held.at[panel, pl.ds(pl.multiple_of(block * rows, rows), rows)], sems.at[panel, block]
        )
        pl.when(last >= info[panel])(copy.wait)


def each_case(info, panel, first, rows, width, grid_rows, load, work):
    top = global_row(first, info[2], grid_rows)
    last = global_row(first + rows - 1, info[2], grid_rows)
    clear = top >= info[panel] + width

    @pl.when(clear)
    def _():
        work(load())

    @pl.when(jnp.logical_not(clear) & (last >= info[panel]))
    def _():
        work(masked(load(), info[panel], info[2], grid_rows, first))


def ring_block(info, step):
    return lax.rem(info[4] + step // 2, 4) * 2 + lax.rem(info[5] + step, 2)


def ring_sources(refs, info):
    return [(ring_block(info, step), [ref.at[k] for k in range(ref.shape[0])]) for step, ref in enumerate(refs)]


def gram_kernel(info, r_ref, *refs, grid_rows):
    *o_refs, total = refs
    panels, rows, width = r_ref.shape
    first = info[3] * rows
    zero, one = [split(masked(r_ref[k], info[k], info[2], grid_rows, first)) for k in range(panels)]
    dims = (((0,), (0,)), ((), ()))

    def dot(left, right):
        return lax.dot_general(left, right, dims, preferred_element_type=F32)

    total[...] = dot(one[0], zero[0]) + (dot(one[0], zero[1]) + dot(one[1], zero[0]))
    part = width // len(o_refs)
    for step, o_ref in enumerate(o_refs):
        at = lax.rem(info[4] + step, len(o_refs)) * part
        o_ref[...] = total[pl.ds(pl.multiple_of(at, part), part), :]


def gram_parts(info, panels, parts, grid_rows):
    width = panels.shape[2]
    return pl.pallas_call(
        lambda *refs: gram_kernel(*refs, grid_rows=grid_rows),
        in_specs=[pl.BlockSpec(memory_space=pltpu.SMEM), pl.BlockSpec(memory_space=pltpu.VMEM)],
        out_specs=[pl.BlockSpec(memory_space=pltpu.VMEM)] * parts,
        out_shape=[jax.ShapeDtypeStruct((width // parts, width), F32)] * parts,
        scratch_shapes=[pltpu.VMEM((width, width), F32)],
        compiler_params=pltpu.CompilerParams(vmem_limit_bytes=16 * 1024 * 1024),
    )(info, panels)


def inner_kernel(info, v_ref, w_ref, *refs, count, parts, grid_rows, chunk):
    r_refs, refs = refs[:count], refs[count:]
    o_refs, (high_ref, low_ref, held, v_held, total, sems, v_sems) = refs[:parts], refs[parts:]
    narrow = v_ref.shape[0]
    panels, depth, width = held.shape
    sources = ring_sources(r_refs, info)
    base = info[3] * depth

    def v_copy(q):
        from_at = pl.ds(pl.multiple_of(base + q * chunk, 128), chunk)
        to_at = pl.ds(pl.multiple_of(q * chunk, 128), chunk)
        return pltpu.make_async_copy(v_ref.at[:, from_at], v_held.at[:, to_at], v_sems.at[q])

    for turn_at, (block, views) in enumerate(sources):
        if turn_at < count - 1:
            v_copy(lax.rem(2 * info[4] + turn_at, count - 1)).start()
        start_block(info, views, held, sems, block, base, grid_rows)
    total[...] = w_ref[...]
    view = sources[0][1][0]
    begin = 2 * info[4]

    def step(done, carry):
        turn_at, k = done // panels, lax.rem(done, panels)
        q = lax.rem(begin + turn_at, count - 1)
        at = pl.multiple_of(q * chunk, chunk)
        first = base + at
        across = pl.ds(pl.multiple_of(k * width, width), width)

        pl.when(k == 0)(v_copy(q).wait)

        @pl.when((k == 0) & ((q == 0) | (turn_at == 0)))
        def _():
            wait_block(info, view, held, sems, q, base, grid_rows)

        @pl.when((k == 0) & (q + 1 != begin))
        def _():
            wait_block(info, view, held, sems, q + 1, base, grid_rows)

        def work(block):
            high, low = split(block)
            high_ref[pl.ds(at, chunk), across] = high
            low_ref[pl.ds(at, chunk), across] = low
            v_high, v_low = split(v_held[:, pl.ds(pl.multiple_of(q * chunk, 128), chunk)])
            both = jnp.concatenate([v_high, v_low], axis=0)
            main = jnp.dot(both, high, preferred_element_type=F32)
            rest = jnp.dot(v_high, low, preferred_element_type=F32)
            total[:, across] += main[:narrow] + (main[narrow:] + rest)

        each_case(info, k, first, chunk, width, grid_rows, lambda: held[k, pl.ds(at, chunk), :], work)
        return carry

    lax.fori_loop(0, (count - 1) * panels, step, 0)
    size = narrow // parts
    for part, o_ref in enumerate(o_refs):
        at = lax.rem(info[6] + part, parts) * size
        o_ref[...] = total[pl.ds(pl.multiple_of(at, size), size), :]


def inner(info, v, start, gathered, parts, shape, grid_rows):
    panels, rows, width = shape
    narrow = v.shape[0]
    count = len(gathered)
    total = count * rows
    vmem = pl.BlockSpec(memory_space=pltpu.VMEM)
    *sums, high, low = pl.pallas_call(
        lambda *refs: inner_kernel(
            *refs, count=count, parts=parts, grid_rows=grid_rows, chunk=total // (count - 1)
        ),
        in_specs=[pl.BlockSpec(memory_space=pltpu.SMEM), pl.BlockSpec(memory_space=pltpu.HBM), vmem]
        + [pl.BlockSpec(memory_space=pltpu.HBM)] * count,
        out_specs=[vmem] * (parts + 2),
        out_shape=[jax.ShapeDtypeStruct((narrow // parts, panels * width), F32)] * parts
        + [jax.ShapeDtypeStruct((total, panels * width), BF16)] * 2,
        scratch_shapes=[
            pltpu.VMEM((panels, total, width), F32),
            pltpu.VMEM((narrow, total), F32),
            pltpu.VMEM((narrow, panels * width), F32),
            pltpu.SemaphoreType.DMA((panels, count)),
            pltpu.SemaphoreType.DMA((count - 1,)),
        ],
        compiler_params=pltpu.CompilerParams(vmem_limit_bytes=22 * 1024 * 1024),
        cost_estimate=pl.CostEstimate(
            flops=6 * narrow * panels * total * width, bytes_accessed=4 * panels * total * width, transcendentals=0
        ),
    )(info, v, start, *gathered)
    return sums, (high, low)


def add_kernel(*refs):
    *parts, o_ref = refs
    total = parts[0][...]
    for part in parts[1:]:
        total += part[...]
    o_ref[...] = total


def add(*parts):
    return pl.pallas_call(
        add_kernel,
        out_shape=jax.ShapeDtypeStruct(parts[0].shape, F32),
        compiler_params=pltpu.CompilerParams(vmem_limit_bytes=2 * 1024 * 1024),
    )(*parts)


def solve_kernel(mine_ref, given_ref, mix_ref, out_ref):
    out_ref[...] = exact_dot(mine_ref[...] + given_ref[...], mix_ref[...])


def solve(mine, given, mix):
    return pl.pallas_call(
        solve_kernel,
        out_shape=jax.ShapeDtypeStruct(mine.shape, F32),
        compiler_params=pltpu.CompilerParams(vmem_limit_bytes=4 * 1024 * 1024),
    )(mine, given, mix)


def turn_kernel(v_ref, o_ref, held, sems, *, chunk):
    steps = o_ref.shape[0] // chunk

    def copy(q):
        at = pl.ds(pl.multiple_of(q * chunk, chunk), chunk)
        return pltpu.make_async_copy(v_ref.at[:, at], held.at[:, at], sems.at[q])

    for q in range(steps):
        copy(q).start()

    def step(q, carry):
        copy(q).wait()
        at = pl.ds(pl.multiple_of(q * chunk, chunk), chunk)
        o_ref[at, :] = held[:, at].T
        return carry

    lax.fori_loop(0, steps, step, 0)


def turn(v, chunk):
    return pl.pallas_call(
        lambda *refs: turn_kernel(*refs, chunk=chunk),
        in_specs=[pl.BlockSpec(memory_space=pltpu.HBM)],
        out_specs=pl.BlockSpec(memory_space=pltpu.VMEM),
        out_shape=jax.ShapeDtypeStruct(v.shape[::-1], F32),
        scratch_shapes=[pltpu.VMEM(v.shape, F32), pltpu.SemaphoreType.DMA((v.shape[1] // chunk,))],
        compiler_params=pltpu.CompilerParams(vmem_limit_bytes=9 * 1024 * 1024),
    )(v)


def mixing_kernel(info, upper_ref, scales_ref, *refs):
    *part_refs, o_ref, gram = refs
    width = gram.shape[0]
    part = width // len(part_refs)
    for step, part_ref in enumerate(part_refs):
        at = lax.rem(info[6] + len(part_refs) - step, len(part_refs)) * part
        gram[pl.ds(pl.multiple_of(at, part), part), :] = part_ref[...]
    row = lax.broadcasted_iota(jnp.int32, (width, width), 0)
    column = lax.broadcasted_iota(jnp.int32, (width, width), 1)

    def factor(k):
        diagonal = jnp.where(row == column, scales_ref[k : k + 1, :], 0.0)
        return jnp.where(row < column, upper_ref[k], diagonal)

    zero, one = factor(0), factor(1)
    corner = exact_dot(one, exact_dot(gram[...], zero))
    o_ref[:width, :width] = zero.T
    o_ref[:width, width:] = -corner.T
    o_ref[width:, :width] = jnp.zeros((width, width), F32)
    o_ref[width:, width:] = one.T


def mixing(info, factor_upper, scales, parts):
    panels, width = scales.shape
    vmem = pl.BlockSpec(memory_space=pltpu.VMEM)
    return pl.pallas_call(
        mixing_kernel,
        in_specs=[pl.BlockSpec(memory_space=pltpu.SMEM)] + [vmem] * (2 + len(parts)),
        out_specs=vmem,
        out_shape=jax.ShapeDtypeStruct((panels * width, panels * width), F32),
        scratch_shapes=[pltpu.VMEM((width, width), F32)],
        compiler_params=pltpu.CompilerParams(vmem_limit_bytes=8 * 1024 * 1024),
    )(info, factor_upper, scales, *parts)


def apply_kernel(info, v_ref, *refs, parts, chunk, grid_rows):
    t_refs, refs = refs[:parts], refs[parts:]
    halves, (o_ref, t_all, t_scr, held, sems) = refs[:4], refs[4:]
    total, depth = halves[0].shape
    panels, width, _ = t_scr.shape
    size = t_refs[0].shape[0]
    narrow = size * parts
    for part, t_ref in enumerate(t_refs):
        at = lax.rem(info[6] + parts - part, parts) * size
        t_all[pl.ds(pl.multiple_of(at, size), size), :] = t_ref[...]
    for k in range(panels):
        high, low = split(t_all[:, k * width : (k + 1) * width].T)
        t_scr[k, :, :narrow] = high
        t_scr[k, :, narrow:] = low
    steps, slots = total // chunk, held.shape[0]

    def copy_of(slot, first):
        return pltpu.make_async_copy(held.at[slot], o_ref.at[pl.ds(first, chunk), :], sems.at[slot])

    for half, (high_ref, low_ref) in enumerate((halves[:2], halves[2:])):
        side = info[3] if half == 0 else 1 - info[3]

        def step(q, carry, half=half, side=side, high_ref=high_ref, low_ref=low_ref):
            at = pl.multiple_of(q * chunk, chunk)
            first = pl.multiple_of(side * total + at, chunk)
            done = half * steps + q
            slot = lax.rem(done, slots)
            pl.when(done >= slots)(copy_of(slot, first).wait)
            held[slot] = v_ref[pl.ds(first, chunk), :]
            last = global_row(first + chunk - 1, info[2], grid_rows)

            def panel(k, carry):
                across = pl.ds(pl.multiple_of(k * width, width), width)

                @pl.when(last >= info[k])
                def _():
                    main = jnp.dot(high_ref[pl.ds(at, chunk), across], t_scr[k], preferred_element_type=F32)
                    rest = jnp.dot(
                        low_ref[pl.ds(at, chunk), across], t_scr[k, :, :narrow], preferred_element_type=F32
                    )
                    held[slot] -= main[:, :narrow] + (main[:, narrow:] + rest)

                return carry

            lax.fori_loop(0, panels, panel, 0)
            copy_of(slot, first).start()
            return carry

        lax.fori_loop(0, steps, step, 0)
    for slot in range(slots):
        copy_of(slot, 0).wait()


def apply(info, v, t, own, other, chunk, grid_rows):
    narrow = v.shape[1]
    depth = t[0].shape[1]
    slots = 7
    vmem = pl.BlockSpec(memory_space=pltpu.VMEM)
    return pl.pallas_call(
        lambda *refs: apply_kernel(*refs, parts=len(t), chunk=chunk, grid_rows=grid_rows),
        in_specs=[pl.BlockSpec(memory_space=pltpu.SMEM)] + [vmem] * (5 + len(t)),
        out_specs=pl.BlockSpec(memory_space=pltpu.HBM),
        out_shape=jax.ShapeDtypeStruct(v.shape, F32),
        scratch_shapes=[
            pltpu.VMEM((narrow, depth), F32),
            pltpu.VMEM((2, depth // 2, 2 * narrow), BF16),
            pltpu.VMEM((slots, chunk, narrow), F32),
            pltpu.SemaphoreType.DMA((slots,)),
        ],
        compiler_params=pltpu.CompilerParams(vmem_limit_bytes=10 * 1024 * 1024),
    )(info, v, *t, *own, *other)


def shards(vectors, panels, offsets, factor_upper, scales):
    grid_rows, grid_cols = lax.axis_size("row"), lax.axis_size("col")
    row_index, col_index = lax.axis_index("row"), lax.axis_index("col")
    half = grid_cols // 2
    rows, width = panels.shape[1:]
    narrow = vectors.shape[1]
    side, ring, core = col_index // half, col_index // 2 % 4, col_index % 2

    def along_col(value, to):
        return lax.ppermute(value, "col", [(c, to(c)) for c in range(grid_cols)])

    def along_row(value, to):
        return lax.ppermute(value, "row", [(r, to(r)) for r in range(grid_rows)])

    def up(c):
        return c // 8 * 8 + (c + 2) % 8

    def down(c):
        return c // 8 * 8 + (c + 6) % 8

    def across(value):
        return along_col(value, lambda c: c ^ 1)

    def info(*ints):
        return jnp.stack([offsets[0], offsets[1]] + [i.astype(jnp.int32) for i in (row_index, *ints)])

    def shifted(step):
        return lambda r: r // 4 * 4 + (r + step) % 4

    def turned(step):
        return lambda c: c // 8 * 8 + (c + 2 * step) % 8

    below, above = along_col(panels, up), along_col(panels, down)
    near = along_col(panels, lambda c: c ^ half)
    panels_across = across(panels)

    dealt = deal(vectors.T, grid_rows)
    level = row_index % 4
    gram, *parts = gram_parts(info(col_index, level), panels, 4, grid_rows)
    gram = sum([along_row(parts[step - 1], shifted(step)) for step in (1, 2, 3)], gram)
    gram = gram.reshape(2, width // 8, width)
    given = across(lax.dynamic_index_in_dim(gram, 1 - core, 0, False))
    gram = lax.dynamic_index_in_dim(gram, core, 0, False) + given
    gram = gram + along_col(gram, lambda c: c ^ half)
    near, below, above, dealt, gram, panels_across = lax.optimization_barrier(
        (near, below, above, dealt, gram, panels_across)
    )

    far = along_col(below, up)
    other_above = along_col(near, down)
    moved = lax.all_to_all(dealt, "row", 0, 0, tiled=True).reshape(grid_rows * narrow, -1)
    crossed = [across(below), across(above), across(near)]
    gram, *crossed = lax.optimization_barrier((gram, *crossed))
    below_across, above_across, near_across = crossed
    gram = sum([along_col(gram, turned(step)) for step in (1, 2, 3)], gram)
    other_above, far, near, gram = lax.optimization_barrier((other_above, far, near, gram))

    other_below, other_far = along_col(near, up), along_col(other_above, down)
    other_above_across, far_across = across(other_above), across(far)
    given = across(gram)
    gram = jnp.where(core == 0, jnp.concatenate([gram, given]), jnp.concatenate([given, gram]))
    gram = gram + along_row(gram, lambda r: r ^ 4)
    own_info, other_info = info(side, ring, core, level), info(1 - side, ring, core, level)
    moved, gram, other_above_across, far_across, own_info, other_info = lax.optimization_barrier(
        (moved, gram, other_above_across, far_across, own_info, other_info)
    )

    moved = pltpu.with_memory_space_constraint(moved, pltpu.HBM)

    chunk = half * rows // (half - 1)
    own = [panels, panels_across, above, above_across, far, far_across, below, below_across]
    own = [pltpu.with_memory_space_constraint(part, pltpu.HBM) for part in own]
    start = jnp.zeros((grid_rows * narrow, 2 * width), F32)
    grams = [gram] + [along_row(gram, shifted(step)) for step in (1, 2, 3)]
    sums, own = inner(own_info, moved, start, own, 1, panels.shape, grid_rows)
    sums, other_far, other_below, *grams = lax.optimization_barrier((*sums, other_far, other_below, *grams))
    other = [near, near_across, other_above, other_above_across, other_far, other_below]
    other = [pltpu.with_memory_space_constraint(part, pltpu.HBM) for part in other]
    other[5:] = [across(other_far), other[5], across(other_below)]
    (mine, *sums), other = inner(other_info, moved, sums, other, 4, panels.shape, grid_rows)

    mine = add(mine, *[along_row(sums[step - 1], shifted(step)) for step in (1, 2, 3)])
    mix = mixing(own_info, factor_upper, scales, grams)
    mine, moved = lax.optimization_barrier((mine, moved))
    current = turn(moved, 896)
    solved = solve(mine, along_row(mine, lambda r: r ^ 4), mix)
    solved = [solved] + [along_row(solved, shifted(step)) for step in (1, 2, 3)]
    return apply(own_info, current, solved, own, other, chunk, grid_rows)


def solution(mesh):
    return jax.shard_map(
        shards,
        mesh=mesh,
        in_specs=(P(None, ("row", "col")), P(None, ("row", "col"), None), P(), P(), P()),
        out_specs=P("row", "col"),
        check_vma=False,
    )
```

```python
import jax
import jax.numpy as jnp
from jax import lax
from jax.experimental import pallas as pl
from jax.experimental.pallas import tpu as pltpu
from jax.sharding import PartitionSpec as P

NB = 64
F32 = jnp.float32
BF16 = jnp.bfloat16


def exact_dot(left, right):
    return jnp.dot(left, right, precision=lax.Precision.HIGHEST, preferred_element_type=F32)


def split(value):
    high = value.astype(BF16)
    return high, (value - high.astype(F32)).astype(BF16)


def masked(block, offset, row_index, grid_rows, first):
    rows, width = block.shape
    position = first + lax.broadcasted_iota(jnp.int32, (rows, 1), 0)
    row = (position // NB * grid_rows + row_index) * NB + position % NB
    begin = offset + lax.broadcasted_iota(jnp.int32, (1, width), 1)
    return jnp.where(row < begin, 0.0, jnp.where(row == begin, 1.0, block))


def deal_kernel(in_ref, out_ref, *, pairs):
    lane = lax.broadcasted_iota(jnp.int32, (in_ref.shape[0], 128), 1)
    low = lane < NB
    for q in range(pairs):
        for t in range(4):
            a = in_ref[:, pl.ds(2 * q * 512 + t * 128, 128)]
            b = in_ref[:, pl.ds((2 * q + 1) * 512 + t * 128, 128)]
            out_ref[2 * t, :, pl.ds(q * 128, 128)] = jnp.where(low, a, pltpu.roll(b, NB, 1))
            out_ref[2 * t + 1, :, pl.ds(q * 128, 128)] = jnp.where(low, pltpu.roll(a, NB, 1), b)


def deal(vectors_t, grid_rows):
    narrow, total = vectors_t.shape
    local = total // grid_rows
    steps = 7
    return pl.pallas_call(
        lambda i, o: deal_kernel(i, o, pairs=local // 128 // steps),
        grid=(steps,),
        in_specs=[pl.BlockSpec((narrow, total // steps), lambda s: (0, s))],
        out_specs=pl.BlockSpec((grid_rows, narrow, local // steps), lambda s: (0, 0, s)),
        out_shape=jax.ShapeDtypeStruct((grid_rows, narrow, local), F32),
    )(vectors_t)


def global_row(position, row_index, grid_rows):
    return (position // NB * grid_rows + row_index) * NB + position % NB


def start_block(info, views, held, sems, block, base, grid_rows):
    rows = views[0].shape[0]
    last = global_row(base + (block + 1) * rows - 1, info[2], grid_rows)
    for panel, view in enumerate(views):
        copy = pltpu.make_async_copy(
            view, held.at[panel, pl.ds(pl.multiple_of(block * rows, rows), rows)], sems.at[panel, block]
        )
        pl.when(last >= info[panel])(copy.start)


def wait_block(info, view, held, sems, block, base, grid_rows):
    rows = view.shape[0]
    last = global_row(base + (block + 1) * rows - 1, info[2], grid_rows)
    for panel in range(held.shape[0]):
        copy = pltpu.make_async_copy(
            view, held.at[panel, pl.ds(pl.multiple_of(block * rows, rows), rows)], sems.at[panel, block]
        )
        pl.when(last >= info[panel])(copy.wait)


def each_case(info, panel, first, rows, width, grid_rows, load, work):
    top = global_row(first, info[2], grid_rows)
    last = global_row(first + rows - 1, info[2], grid_rows)
    clear = top >= info[panel] + width

    @pl.when(clear)
    def _():
        work(load())

    @pl.when(jnp.logical_not(clear) & (last >= info[panel]))
    def _():
        work(masked(load(), info[panel], info[2], grid_rows, first))


def ring_block(info, step):
    return lax.rem(info[4] + step // 2, 4) * 2 + lax.rem(info[5] + step, 2)


def ring_sources(refs, info):
    return [(ring_block(info, step), [ref.at[k] for k in range(ref.shape[0])]) for step, ref in enumerate(refs)]


def gram_kernel(info, r_ref, *refs, grid_rows):
    *o_refs, total = refs
    panels, rows, width = r_ref.shape
    first = info[3] * rows
    zero, one = [split(masked(r_ref[k], info[k], info[2], grid_rows, first)) for k in range(panels)]
    dims = (((0,), (0,)), ((), ()))

    def dot(left, right):
        return lax.dot_general(left, right, dims, preferred_element_type=F32)

    total[...] = dot(one[0], zero[0]) + (dot(one[0], zero[1]) + dot(one[1], zero[0]))
    part = width // len(o_refs)
    for step, o_ref in enumerate(o_refs):
        at = lax.rem(info[4] + step, len(o_refs)) * part
        o_ref[...] = total[pl.ds(pl.multiple_of(at, part), part), :]


def gram_parts(info, panels, parts, grid_rows):
    width = panels.shape[2]
    return pl.pallas_call(
        lambda *refs: gram_kernel(*refs, grid_rows=grid_rows),
        in_specs=[pl.BlockSpec(memory_space=pltpu.SMEM), pl.BlockSpec(memory_space=pltpu.VMEM)],
        out_specs=[pl.BlockSpec(memory_space=pltpu.VMEM)] * parts,
        out_shape=[jax.ShapeDtypeStruct((width // parts, width), F32)] * parts,
        scratch_shapes=[pltpu.VMEM((width, width), F32)],
        compiler_params=pltpu.CompilerParams(vmem_limit_bytes=16 * 1024 * 1024),
    )(info, panels)


def inner_kernel(info, v_ref, w_ref, *refs, count, parts, grid_rows, chunk):
    r_refs, refs = refs[:count], refs[count:]
    o_refs, (high_ref, low_ref, held, v_held, total, sems, v_sems) = refs[:parts], refs[parts:]
    narrow = v_ref.shape[0]
    panels, depth, width = held.shape
    sources = ring_sources(r_refs, info)
    base = info[3] * depth

    def v_copy(q):
        from_at = pl.ds(pl.multiple_of(base + q * chunk, 128), chunk)
        to_at = pl.ds(pl.multiple_of(q * chunk, 128), chunk)
        return pltpu.make_async_copy(v_ref.at[:, from_at], v_held.at[:, to_at], v_sems.at[q])

    for turn_at, (block, views) in enumerate(sources):
        if turn_at < count - 1:
            v_copy(lax.rem(2 * info[4] + turn_at, count - 1)).start()
        start_block(info, views, held, sems, block, base, grid_rows)
    total[...] = w_ref[...]
    view = sources[0][1][0]
    begin = 2 * info[4]

    def step(done, carry):
        turn_at, k = done // panels, lax.rem(done, panels)
        q = lax.rem(begin + turn_at, count - 1)
        at = pl.multiple_of(q * chunk, chunk)
        first = base + at
        across = pl.ds(pl.multiple_of(k * width, width), width)

        pl.when(k == 0)(v_copy(q).wait)

        @pl.when((k == 0) & ((q == 0) | (turn_at == 0)))
        def _():
            wait_block(info, view, held, sems, q, base, grid_rows)

        @pl.when((k == 0) & (q + 1 != begin))
        def _():
            wait_block(info, view, held, sems, q + 1, base, grid_rows)

        def work(block):
            high, low = split(block)
            high_ref[pl.ds(at, chunk), across] = high
            low_ref[pl.ds(at, chunk), across] = low
            v_high, v_low = split(v_held[:, pl.ds(pl.multiple_of(q * chunk, 128), chunk)])
            both = jnp.concatenate([v_high, v_low], axis=0)
            main = jnp.dot(both, high, preferred_element_type=F32)
            rest = jnp.dot(v_high, low, preferred_element_type=F32)
            total[:, across] += main[:narrow] + (main[narrow:] + rest)

        each_case(info, k, first, chunk, width, grid_rows, lambda: held[k, pl.ds(at, chunk), :], work)
        return carry

    lax.fori_loop(0, (count - 1) * panels, step, 0)
    size = narrow // parts
    for part, o_ref in enumerate(o_refs):
        at = lax.rem(info[6] + part, parts) * size
        o_ref[...] = total[pl.ds(pl.multiple_of(at, size), size), :]


def inner(info, v, start, gathered, parts, shape, grid_rows):
    panels, rows, width = shape
    narrow = v.shape[0]
    count = len(gathered)
    total = count * rows
    vmem = pl.BlockSpec(memory_space=pltpu.VMEM)
    *sums, high, low = pl.pallas_call(
        lambda *refs: inner_kernel(
            *refs, count=count, parts=parts, grid_rows=grid_rows, chunk=total // (count - 1)
        ),
        in_specs=[pl.BlockSpec(memory_space=pltpu.SMEM), pl.BlockSpec(memory_space=pltpu.HBM), vmem]
        + [pl.BlockSpec(memory_space=pltpu.HBM)] * count,
        out_specs=[vmem] * (parts + 2),
        out_shape=[jax.ShapeDtypeStruct((narrow // parts, panels * width), F32)] * parts
        + [jax.ShapeDtypeStruct((total, panels * width), BF16)] * 2,
        scratch_shapes=[
            pltpu.VMEM((panels, total, width), F32),
            pltpu.VMEM((narrow, total), F32),
            pltpu.VMEM((narrow, panels * width), F32),
            pltpu.SemaphoreType.DMA((panels, count)),
            pltpu.SemaphoreType.DMA((count - 1,)),
        ],
        compiler_params=pltpu.CompilerParams(vmem_limit_bytes=22 * 1024 * 1024),
        cost_estimate=pl.CostEstimate(
            flops=6 * narrow * panels * total * width, bytes_accessed=4 * panels * total * width, transcendentals=0
        ),
    )(info, v, start, *gathered)
    return sums, (high, low)


def add_kernel(*refs):
    *parts, o_ref = refs
    total = parts[0][...]
    for part in parts[1:]:
        total += part[...]
    o_ref[...] = total


def add(*parts):
    return pl.pallas_call(
        add_kernel,
        out_shape=jax.ShapeDtypeStruct(parts[0].shape, F32),
        compiler_params=pltpu.CompilerParams(vmem_limit_bytes=2 * 1024 * 1024),
    )(*parts)


def solve_kernel(mine_ref, given_ref, mix_ref, out_ref):
    out_ref[...] = exact_dot(mine_ref[...] + given_ref[...], mix_ref[...])


def solve(mine, given, mix):
    return pl.pallas_call(
        solve_kernel,
        out_shape=jax.ShapeDtypeStruct(mine.shape, F32),
        compiler_params=pltpu.CompilerParams(vmem_limit_bytes=4 * 1024 * 1024),
    )(mine, given, mix)


def turn_kernel(v_ref, o_ref, held, sems, *, chunk):
    steps = o_ref.shape[0] // chunk

    def copy(q):
        at = pl.ds(pl.multiple_of(q * chunk, chunk), chunk)
        return pltpu.make_async_copy(v_ref.at[:, at], held.at[:, at], sems.at[q])

    for q in range(steps):
        copy(q).start()

    def step(q, carry):
        copy(q).wait()
        at = pl.ds(pl.multiple_of(q * chunk, chunk), chunk)
        o_ref[at, :] = held[:, at].T
        return carry

    lax.fori_loop(0, steps, step, 0)


def turn(v, chunk):
    return pl.pallas_call(
        lambda *refs: turn_kernel(*refs, chunk=chunk),
        in_specs=[pl.BlockSpec(memory_space=pltpu.HBM)],
        out_specs=pl.BlockSpec(memory_space=pltpu.VMEM),
        out_shape=jax.ShapeDtypeStruct(v.shape[::-1], F32),
        scratch_shapes=[pltpu.VMEM(v.shape, F32), pltpu.SemaphoreType.DMA((v.shape[1] // chunk,))],
        compiler_params=pltpu.CompilerParams(vmem_limit_bytes=9 * 1024 * 1024),
    )(v)


def mixing_kernel(info, upper_ref, scales_ref, *refs):
    *part_refs, o_ref, gram = refs
    width = gram.shape[0]
    part = width // len(part_refs)
    for step, part_ref in enumerate(part_refs):
        at = lax.rem(info[6] + len(part_refs) - step, len(part_refs)) * part
        gram[pl.ds(pl.multiple_of(at, part), part), :] = part_ref[...]
    row = lax.broadcasted_iota(jnp.int32, (width, width), 0)
    column = lax.broadcasted_iota(jnp.int32, (width, width), 1)

    def factor(k):
        diagonal = jnp.where(row == column, scales_ref[k : k + 1, :], 0.0)
        return jnp.where(row < column, upper_ref[k], diagonal)

    zero, one = factor(0), factor(1)
    corner = exact_dot(one, exact_dot(gram[...], zero))
    o_ref[:width, :width] = zero.T
    o_ref[:width, width:] = -corner.T
    o_ref[width:, :width] = jnp.zeros((width, width), F32)
    o_ref[width:, width:] = one.T


def mixing(info, factor_upper, scales, parts):
    panels, width = scales.shape
    vmem = pl.BlockSpec(memory_space=pltpu.VMEM)
    return pl.pallas_call(
        mixing_kernel,
        in_specs=[pl.BlockSpec(memory_space=pltpu.SMEM)] + [vmem] * (2 + len(parts)),
        out_specs=vmem,
        out_shape=jax.ShapeDtypeStruct((panels * width, panels * width), F32),
        scratch_shapes=[pltpu.VMEM((width, width), F32)],
        compiler_params=pltpu.CompilerParams(vmem_limit_bytes=8 * 1024 * 1024),
    )(info, factor_upper, scales, *parts)


def apply_kernel(info, v_ref, *refs, parts, chunk, grid_rows):
    t_refs, refs = refs[:parts], refs[parts:]
    halves, (o_ref, t_all, t_scr, held, sems) = refs[:4], refs[4:]
    total, depth = halves[0].shape
    panels, width = 2, depth // 2
    size = t_refs[0].shape[0]
    narrow = size * parts
    for part, t_ref in enumerate(t_refs):
        at = lax.rem(info[6] + parts - part, parts) * size
        t_all[pl.ds(pl.multiple_of(at, size), size), :] = t_ref[...]
    for k in range(panels):
        high, low = split(t_all[:, k * width : (k + 1) * width].T)
        t_scr[k * width : (k + 1) * width, :narrow] = high
        t_scr[k * width : (k + 1) * width, narrow:] = low
    steps, slots = total // chunk, held.shape[0]

    def copy_of(slot, first):
        return pltpu.make_async_copy(held.at[slot], o_ref.at[pl.ds(first, chunk), :], sems.at[slot])

    for half, (high_ref, low_ref) in enumerate((halves[:2], halves[2:])):
        side = info[3] if half == 0 else 1 - info[3]

        def step(q, carry, half=half, side=side, high_ref=high_ref, low_ref=low_ref):
            at = pl.multiple_of(q * chunk, chunk)
            first = pl.multiple_of(side * total + at, chunk)
            done = half * steps + q
            slot = lax.rem(done, slots)
            pl.when(done >= slots)(copy_of(slot, first).wait)
            held[slot] = v_ref[pl.ds(first, chunk), :]
            last = global_row(first + chunk - 1, info[2], grid_rows)

            def lessen(across):
                main = jnp.dot(high_ref[pl.ds(at, chunk), across], t_scr[across, :], preferred_element_type=F32)
                rest = jnp.dot(
                    low_ref[pl.ds(at, chunk), across], t_scr[across, :narrow], preferred_element_type=F32
                )
                held[slot] -= main[:, :narrow] + (main[:, narrow:] + rest)

            every = (last >= info[0]) & (last >= info[1])
            pl.when(every)(lambda: lessen(pl.ds(0, depth)))
            k = jnp.where(last >= info[0], 0, 1)

            @pl.when(jnp.logical_not(every) & (last >= info[k]))
            def _():
                lessen(pl.ds(pl.multiple_of(k * width, width), width))

            copy_of(slot, first).start()
            return carry

        lax.fori_loop(0, steps, step, 0)
    for slot in range(slots):
        copy_of(slot, 0).wait()


def apply(info, v, t, own, other, chunk, grid_rows):
    narrow = v.shape[1]
    depth = t[0].shape[1]
    slots = 7
    vmem = pl.BlockSpec(memory_space=pltpu.VMEM)
    return pl.pallas_call(
        lambda *refs: apply_kernel(*refs, parts=len(t), chunk=chunk, grid_rows=grid_rows),
        in_specs=[pl.BlockSpec(memory_space=pltpu.SMEM)] + [vmem] * (5 + len(t)),
        out_specs=pl.BlockSpec(memory_space=pltpu.HBM),
        out_shape=jax.ShapeDtypeStruct(v.shape, F32),
        scratch_shapes=[
            pltpu.VMEM((narrow, depth), F32),
            pltpu.VMEM((depth, 2 * narrow), BF16),
            pltpu.VMEM((slots, chunk, narrow), F32),
            pltpu.SemaphoreType.DMA((slots,)),
        ],
        compiler_params=pltpu.CompilerParams(vmem_limit_bytes=10 * 1024 * 1024),
    )(info, v, *t, *own, *other)


def shards(vectors, panels, offsets, factor_upper, scales):
    grid_rows, grid_cols = lax.axis_size("row"), lax.axis_size("col")
    row_index, col_index = lax.axis_index("row"), lax.axis_index("col")
    half = grid_cols // 2
    rows, width = panels.shape[1:]
    narrow = vectors.shape[1]
    side, ring, core = col_index // half, col_index // 2 % 4, col_index % 2

    def along_col(value, to):
        return lax.ppermute(value, "col", [(c, to(c)) for c in range(grid_cols)])

    def along_row(value, to):
        return lax.ppermute(value, "row", [(r, to(r)) for r in range(grid_rows)])

    def up(c):
        return c // 8 * 8 + (c + 2) % 8

    def down(c):
        return c // 8 * 8 + (c + 6) % 8

    def across(value):
        return along_col(value, lambda c: c ^ 1)

    def info(*ints):
        return jnp.stack([offsets[0], offsets[1]] + [i.astype(jnp.int32) for i in (row_index, *ints)])

    def shifted(step):
        return lambda r: r // 4 * 4 + (r + step) % 4

    def turned(step):
        return lambda c: c // 8 * 8 + (c + 2 * step) % 8

    below, above = along_col(panels, up), along_col(panels, down)
    near = along_col(panels, lambda c: c ^ half)
    panels_across = across(panels)

    dealt = deal(vectors.T, grid_rows)
    level = row_index % 4
    gram, *parts = gram_parts(info(col_index, level), panels, 4, grid_rows)
    gram = sum([along_row(parts[step - 1], shifted(step)) for step in (1, 2, 3)], gram)
    gram = gram.reshape(2, width // 8, width)
    given = across(lax.dynamic_index_in_dim(gram, 1 - core, 0, False))
    gram = lax.dynamic_index_in_dim(gram, core, 0, False) + given
    gram = gram + along_col(gram, lambda c: c ^ half)
    near, below, above, dealt, gram, panels_across = lax.optimization_barrier(
        (near, below, above, dealt, gram, panels_across)
    )

    far = along_col(below, up)
    other_above = along_col(near, down)
    moved = lax.all_to_all(dealt, "row", 0, 0, tiled=True).reshape(grid_rows * narrow, -1)
    crossed = [across(below), across(above), across(near)]
    gram, *crossed = lax.optimization_barrier((gram, *crossed))
    below_across, above_across, near_across = crossed
    gram = sum([along_col(gram, turned(step)) for step in (1, 2, 3)], gram)
    other_above, far, near, gram = lax.optimization_barrier((other_above, far, near, gram))

    other_below, other_far = along_col(near, up), along_col(other_above, down)
    other_above_across, far_across = across(other_above), across(far)
    given = across(gram)
    gram = jnp.where(core == 0, jnp.concatenate([gram, given]), jnp.concatenate([given, gram]))
    gram = gram + along_row(gram, lambda r: r ^ 4)
    own_info, other_info = info(side, ring, core, level), info(1 - side, ring, core, level)
    moved, gram, other_above_across, far_across, own_info, other_info = lax.optimization_barrier(
        (moved, gram, other_above_across, far_across, own_info, other_info)
    )

    moved = pltpu.with_memory_space_constraint(moved, pltpu.HBM)

    chunk = half * rows // (half - 1)
    own = [panels, panels_across, above, above_across, far, far_across, below, below_across]
    own = [pltpu.with_memory_space_constraint(part, pltpu.HBM) for part in own]
    start = jnp.zeros((grid_rows * narrow, 2 * width), F32)
    grams = [gram] + [along_row(gram, shifted(step)) for step in (1, 2, 3)]
    sums, own = inner(own_info, moved, start, own, 1, panels.shape, grid_rows)
    sums, other_far, other_below, *grams = lax.optimization_barrier((*sums, other_far, other_below, *grams))
    other = [near, near_across, other_above, other_above_across, other_far, other_below]
    other = [pltpu.with_memory_space_constraint(part, pltpu.HBM) for part in other]
    other[5:] = [across(other_far), other[5], across(other_below)]
    (mine, *sums), other = inner(other_info, moved, sums, other, 4, panels.shape, grid_rows)

    mine = add(mine, *[along_row(sums[step - 1], shifted(step)) for step in (1, 2, 3)])
    mix = mixing(own_info, factor_upper, scales, grams)
    mine, moved = lax.optimization_barrier((mine, moved))
    current = turn(moved, 896)
    solved = solve(mine, along_row(mine, lambda r: r ^ 4), mix)
    solved = [solved] + [along_row(solved, shifted(step)) for step in (1, 2, 3)]
    return apply(own_info, current, solved, own, other, chunk, grid_rows)


def solution(mesh):
    return jax.shard_map(
        shards,
        mesh=mesh,
        in_specs=(P(None, ("row", "col")), P(None, ("row", "col"), None), P(), P(), P()),
        out_specs=P("row", "col"),
        check_vma=False,
    )
```
